32 devices in a mesh: seq: 16 (over z, y, x), tp: 2 (over core).
Axes of the slice: x: 2, y: 2, z: 4, core: 2. Of those that a mesh axis runs over, the one named last changes fastest.
Arguments:
- query_rows: bfloat16 [8192, 1536], P('seq', 'tp'), may hold values from -48 to 48
- key_rows: bfloat16 [8192, 1536], P('seq', 'tp'), may hold values from -8 to 8
- value_rows: bfloat16 [8192, 1536], P('seq', 'tp'), may hold values from -6 to 6
- frame_counts: int32 [12], replicated, may hold values from 1 to 4, 32 in all
- out_weight: bfloat16 [1536, 3072], P('tp'), may hold values from -0.15625 to 0.15625
Outputs:
- mixed: bfloat16 [8192, 3072], P('seq', 'tp')
The draws below stay inside these ranges and needn't reach their ends.
Inputs may be any that keep to these rules, and one draw needn't show every extreme that they name: `frame_counts`: the 12 clips' frame counts sum to 32; the longest has exactly 4 frames.
All inputs are finite; a program needn't handle non-finite values.
Results may differ from the reference program's by a relative error of at most 0.015.
Values may be sent and summed in bfloat16 or wider, within the bound.
A program may use at most 64 MiB of HBM per device.

```python
import math
import jax
import jax.numpy as jnp
import numpy as np
from jax import lax

D = 3072
HEADS = 12
RT = 16
RH = 56
RW = 56
PH = 16
PW = 16
CLIPS = 12
TOK_DEV = 512
HEAD_DIM = 128
TOKENS = 8192
FRAME = 256
FRAMES = 32
CLIP_MOST = 4


def sign_table(key):
    flips = jax.random.bernoulli(jax.random.fold_in(key, 11), 0.5, (TOKENS, HEADS * HEAD_DIM))
    return jnp.where(flips, 1.0, -1.0).astype(jnp.float32)


def draw_key_rows(key, part):
    sign_rows = sign_table(key)
    key = jax.random.fold_in(key, 1)
    extent = (TOKENS, HEADS * HEAD_DIM)
    fresh = jnp.clip(1.6 * jax.random.normal(key, extent, jnp.float32), -8.0, 8.0)
    row_phase = (jnp.arange(TOKENS, dtype=jnp.int32) % 64)[:, None]
    lead_column = (jnp.arange(HEADS * HEAD_DIM, dtype=jnp.int32) % HEAD_DIM == 0)[None, :]
    earlier_signs = jnp.roll(sign_rows, 1, axis=0)
    twin_row = jnp.where(lead_column, 0.0, 1.6 * earlier_signs)
    drawn = jnp.where(row_phase == 5, 1.6 * sign_rows, jnp.where(row_phase == 6, twin_row, fresh))
    return drawn.astype(jnp.bfloat16)


def draw_query_rows(key, part):
    key = jax.random.fold_in(key, 2)
    extent = (TOKENS, HEADS * HEAD_DIM)
    drawn = jnp.clip(1.6 * jax.random.normal(key, extent, jnp.float32), -8.0, 8.0)
    return drawn.astype(jnp.bfloat16)


def levels(key, shape, cuts, low, top_value):
    gain, own = 1.0, jax.random.fold_in(key, 6)
    for dim, parts in cuts:
        steps = jnp.exp(jax.random.uniform(jax.random.fold_in(own, dim), (parts,), jnp.float32, low / len(cuts), top_value / len(cuts)))
        gain = gain * jnp.repeat(steps, shape[dim] // parts).reshape([-1 if axis == dim else 1 for axis in range(len(shape))])
    return gain


def profile(amount, total, limit, skew):
    weights = [(1 << 20) // math.isqrt(rank ** skew) + 1 for rank in range(2, amount + 1)]
    rest, holding = total - limit - (amount - 1), [1] * (amount - 1)
    while rest > 0:
        movable = [i for i in range(amount - 1) if holding[i] < limit]
        whole, left = sum([weights[i] for i in movable]), rest
        for i in movable:
            extra = min(limit - holding[i], max(1, left * weights[i] // whole), rest)
            holding[i] = holding[i] + extra
            rest = rest - extra
    return np.array([limit] + holding)


def uneven(key, number_of, total, reach, skew):
    if number_of == 2:
        one = jax.random.randint(key, (), max(1, total - reach), min(reach, total - 1) + 1)
        return jnp.stack([one, total - one])
    tallies = jnp.asarray(profile(number_of, total, reach, skew), jnp.int32)
    couples = (number_of - 1) // 2
    giver, taker = tallies[1:1 + 2 * couples:2], tallies[2:2 + 2 * couples:2]
    room = jnp.minimum(giver - 1, reach - taker)
    moved = jax.random.randint(jax.random.fold_in(key, 1), (couples,), 0, 1 << 20) % (room + 1)
    tallies = tallies.at[1:1 + 2 * couples:2].set(giver - moved).at[2:2 + 2 * couples:2].set(taker + moved)
    return tallies[jax.random.permutation(jax.random.fold_in(key, 2), number_of)]


def centred(own_key, dims, spread, reach, split=(), kind=jnp.bfloat16):
    gain = levels(own_key, dims, split, -0.22, 0.18) if split else 1.0
    values = jax.random.normal(own_key, dims, jnp.float32) * spread * gain
    return jnp.minimum(jnp.maximum(values, -reach), reach).astype(kind)


def setup_inputs(seed: int = 0) -> dict:
    keys = jax.random.split(jax.random.key(seed), 6)
    query_rows = draw_query_rows(jax.random.fold_in(keys[5], 71), 0)
    key_rows = draw_key_rows(jax.random.fold_in(keys[5], 71), 0)
    value_rows = centred(keys[2], (TOKENS, HEADS * HEAD_DIM), 1.0, 6.0, ((0, 16), (1, 2)))
    frame_counts = uneven(keys[3], CLIPS, FRAMES, CLIP_MOST, 2).astype(jnp.int32)
    out_weight = centred(keys[4], (HEADS * HEAD_DIM, D), (HEADS * HEAD_DIM) ** -0.5, 0.15625, ((0, 2),))
    return {"query_rows": query_rows, "key_rows": key_rows, "value_rows": value_rows, "frame_counts": frame_counts, "out_weight": out_weight}


NEG_FILL = -1e30
ROPE_BASE = 256.0


def clip_layout(frame_counts, token_index):
    clip_sizes = frame_counts * (PH * PW)
    clip_ends = jnp.cumsum(clip_sizes)
    passed = token_index[:, None] >= clip_ends[None, :]
    clip_id = jnp.sum(passed.astype(jnp.int32), axis=1)
    clip_start = jnp.sum(jnp.where(passed, clip_sizes[None, :], 0), axis=1)
    return clip_id, token_index - clip_start


def rotate(features, offset):
    frame_size = PH * PW
    coordinates = (offset // frame_size, (offset % frame_size) // PW, offset % PW)
    pieces = []
    section_start = 0
    for section_width, coordinate in zip((RT, RH, RW), coordinates):
        half_width = section_width // 2
        section = features[:, :, section_start:section_start + section_width]
        first_half = section[..., :half_width]
        second_half = section[..., half_width:]
        frequency = jnp.exp(-(2.0 * jnp.arange(half_width, dtype=jnp.float32) / section_width) * math.log(ROPE_BASE))
        phase_angle = coordinate.astype(jnp.float32)[:, None] * frequency[None, :]
        cosine = jnp.cos(phase_angle)[:, None, :]
        sine_part = jnp.sin(phase_angle)[:, None, :]
        pieces.append(first_half * cosine - second_half * sine_part)
        pieces.append(second_half * cosine + first_half * sine_part)
        section_start = section_start + section_width
    return jnp.concatenate(pieces, axis=2)


def reference(query_rows, key_rows, value_rows, frame_counts, out_weight):
    token_index = jnp.arange(TOKENS, dtype=jnp.int32)
    clip_id, offset = clip_layout(frame_counts, token_index)
    rotated_q = rotate(query_rows.astype(jnp.float32).reshape(TOKENS, HEADS, HEAD_DIM), offset).astype(jnp.bfloat16)
    rotated_k = rotate(key_rows.astype(jnp.float32).reshape(TOKENS, HEADS, HEAD_DIM), offset).astype(jnp.bfloat16)
    rotated_q = lax.optimization_barrier(rotated_q)
    rotated_k = lax.optimization_barrier(rotated_k)
    value_heads = value_rows.reshape(TOKENS, HEADS, HEAD_DIM)
    reach_tokens = CLIP_MOST * FRAME
    key_padded = jnp.pad(rotated_k, ((reach_tokens, reach_tokens), (0, 0), (0, 0)))
    value_padded = jnp.pad(value_heads, ((reach_tokens, reach_tokens), (0, 0), (0, 0)))
    clip_padded = jnp.pad(clip_id, (reach_tokens, reach_tokens), constant_values=-1)
    span_tokens = TOK_DEV + 2 * reach_tokens
    scale_factor = HEAD_DIM ** -0.5

    def block(block_index):
        lower = (block_index * TOK_DEV).astype(jnp.int32)
        query_block = lax.dynamic_slice_in_dim(rotated_q, lower, TOK_DEV, 0).astype(jnp.float32)
        key_block = lax.dynamic_slice_in_dim(key_padded, lower, span_tokens, 0).astype(jnp.float32)
        value_block = lax.dynamic_slice_in_dim(value_padded, lower, span_tokens, 0).astype(jnp.float32)
        query_clip = lax.dynamic_slice_in_dim(clip_id, lower, TOK_DEV, 0)
        key_clip = lax.dynamic_slice_in_dim(clip_padded, lower, span_tokens, 0)
        scores = jnp.einsum("qhd,khd->hqk", query_block, key_block) * scale_factor
        allowed = query_clip[:, None] == key_clip[None, :]
        scores = jnp.where(allowed[None], scores, NEG_FILL)
        row_max = jnp.max(scores, axis=2, keepdims=True)
        expo = jnp.where(allowed[None], jnp.exp(scores - row_max), 0.0)
        total = jnp.sum(expo, axis=2)
        weights = lax.optimization_barrier(expo.astype(jnp.bfloat16)).astype(jnp.float32)
        summed = jnp.einsum("hqk,khd->hqd", weights, value_block) / total[:, :, None]
        return summed.transpose(1, 0, 2).reshape(TOK_DEV, HEADS * HEAD_DIM).astype(jnp.bfloat16)

    attended = lax.map(block, jnp.arange(TOKENS // TOK_DEV, dtype=jnp.int32)).reshape(TOKENS, HEADS * HEAD_DIM)
    return jnp.dot(attended, out_weight, preferred_element_type=jnp.float32).astype(jnp.bfloat16)
```

```python
import functools
import math

import jax
import jax.numpy as jnp
import numpy as np
from jax import lax
from jax.experimental import pallas as pl
from jax.experimental.pallas import tpu as pltpu
from jax.sharding import PartitionSpec as P

SECTIONS = (16, 56, 56)
PH = 16
PW = 16
FRAME = PH * PW
HEAD_DIM = 128
ROPE_BASE = 256.0
NEG_FILL = -1e30
MESH = pl.DeviceIdType.MESH


def rope_tables(longest):
    angle_hw = np.zeros((FRAME, HEAD_DIM), np.float64)
    angle_t = np.zeros((longest, HEAD_DIM), np.float64)
    pairing = np.zeros((HEAD_DIM, HEAD_DIM), np.float32)
    row = np.arange(FRAME)
    first = 0
    for section, width in enumerate(SECTIONS):
        half = width // 2
        frequency = np.exp(-(2.0 * np.arange(half) / width) * math.log(ROPE_BASE))
        frequency = np.concatenate([frequency, frequency])
        lanes = slice(first, first + width)
        if section == 0:
            angle_t[:, lanes] = np.arange(longest)[:, None] * frequency[None, :]
        else:
            place = row // PW if section == 1 else row % PW
            angle_hw[:, lanes] = place[:, None] * frequency[None, :]
        for j in range(half):
            pairing[first + half + j, first + j] = -1.0
            pairing[first + j, first + half + j] = 1.0
        first += width
    angle_t = angle_t[:, None, :]
    tables = [np.cos(angle_hw), np.sin(angle_hw), np.cos(angle_t), np.sin(angle_t)]
    return [jnp.asarray(table, jnp.float32) for table in tables] + [
        jnp.asarray(pairing, jnp.bfloat16)
    ]


def clip_span(counts_ref, clips, longest, frame):
    start = jnp.int32(0)
    stop = jnp.int32(1 << 30)
    end = jnp.int32(0)
    for clip in range(clips):
        end = end + counts_ref[clip]
        start = jnp.where(end <= frame, end, start)
        stop = jnp.where(end > frame, jnp.minimum(stop, end), stop)
    return jnp.clip(start, frame - (longest - 1), frame), stop


def kernel(
    dims,
    counts_ref,
    q_ref,
    k_ref,
    v_ref,
    w_ref,
    cos_hw,
    sin_hw,
    cos_t,
    sin_t,
    pairing,
    out_ref,
    q_own,
    kv_own,
    q_all,
    kv_all,
    o_mine,
    o_all,
    w_all,
    total_ref,
    w_local,
    w_send,
    w_recv,
    kv_send,
    kv_recv,
    q_send,
    q_recv,
    halo_send,
    halo_recv,
    o_send,
    o_recv,
    x_send,
    x_recv,
):
    heads, group, groups, peers, slots, longest, clips, own_frames = dims
    rows = own_frames * FRAME
    halo = longest - 1
    span = group * own_frames
    reach = (halo + span - 1) // span
    columns = out_ref.shape[1]
    position = lax.axis_index("seq")
    tp = lax.axis_index("tp")
    plane = position // group
    member = position % group
    first_frame = plane * span

    def head_of(who, slot):
        return lax.rem(who - 2 * tp + 2 * group * peers, group) + slot * group

    def sized(slot):
        return min(group, heads - slot * group)

    def to_member(d):
        return lax.rem(member + d, group)

    def from_member(d):
        return lax.rem(member - d + group, group)

    def device(seq, core):
        return (seq, core)

    barrier = pltpu.get_barrier_semaphore()
    for d in range(1, group):
        pl.semaphore_signal(
            barrier, inc=1, device_id=device(plane * group + to_member(d), tp), device_id_type=MESH
        )
    for d in range(1, peers):
        pl.semaphore_signal(
            barrier, inc=1, device_id=device(position, lax.rem(tp + d, peers)), device_id_type=MESH
        )
    greeted = jnp.int32(group - 1 + peers - 1)
    for d in range(1, reach + 1):
        above = plane + d < groups
        below = plane - d >= 0

        @pl.when(above)
        def _():
            pl.semaphore_signal(
                barrier, inc=1, device_id=device(position + d * group, tp), device_id_type=MESH
            )

        @pl.when(below)
        def _():
            pl.semaphore_signal(
                barrier, inc=1, device_id=device(position - d * group, tp), device_id_type=MESH
            )

        greeted = greeted + above.astype(jnp.int32) + below.astype(jnp.int32)
    pl.semaphore_wait(barrier, greeted)

    lane = lax.broadcasted_iota(jnp.int32, (FRAME, HEAD_DIM), 1)
    in_t = lane < SECTIONS[0]
    cosines, sines = [], []
    for f in range(own_frames):
        frame = position * own_frames + f
        t = frame - clip_span(counts_ref, clips, longest, frame)[0]
        cosines.append(jnp.where(in_t, cos_t[t], cos_hw[...]))
        sines.append(jnp.where(in_t, sin_t[t], sin_hw[...]))

    def rotated(ref, f, head):
        x = ref[f * FRAME : (f + 1) * FRAME, head * HEAD_DIM : (head + 1) * HEAD_DIM]
        paired = jnp.dot(x, pairing[...], preferred_element_type=jnp.float32)
        return (x.astype(jnp.float32) * cosines[f] + paired * sines[f]).astype(jnp.bfloat16)

    def own_rows(who):
        return pl.ds(halo + who * own_frames, own_frames)

    def query_rows(who):
        return pl.ds(pl.multiple_of(who * rows, rows), rows)

    def kv_copy(slot, d, source, target):
        return pltpu.make_async_remote_copy(
            src_ref=kv_own.at[head_of(target, slot)],
            dst_ref=kv_all[slot].at[:, own_rows(source)],
            send_sem=kv_send.at[slot, d],
            recv_sem=kv_recv.at[slot, d],
            device_id=device(plane * group + target, tp),
            device_id_type=MESH,
        )

    def q_copy(slot, d, source, target):
        return pltpu.make_async_remote_copy(
            src_ref=q_own.at[head_of(target, slot)],
            dst_ref=q_all.at[slot, query_rows(source), :],
            send_sem=q_send.at[slot, d],
            recv_sem=q_recv.at[slot, d],
            device_id=device(plane * group + target, tp),
            device_id_type=MESH,
        )

    def o_copy(slot, d, source, target):
        return pltpu.make_async_remote_copy(
            src_ref=o_mine.at[slot, query_rows(target), :],
            dst_ref=o_all.at[tp, head_of(source, slot)],
            send_sem=o_send.at[slot, d],
            recv_sem=o_recv.at[slot, d],
            device_id=device(plane * group + target, tp),
            device_id_type=MESH,
        )

    def w_copy(d):
        target = lax.rem(tp + d, peers)
        return pltpu.make_async_remote_copy(
            src_ref=w_ref.at[:, pl.ds(pl.multiple_of(target * columns, columns), columns)],
            dst_ref=w_all.at[tp],
            send_sem=w_send.at[d],
            recv_sem=w_recv.at[d],
            device_id=device(position, target),
            device_id_type=MESH,
        )

    def w_arrival(d):
        source = lax.rem(tp - d + peers, peers)
        return pltpu.make_async_remote_copy(
            src_ref=w_ref.at[:, pl.ds(pl.multiple_of(tp * columns, columns), columns)],
            dst_ref=w_all.at[source],
            send_sem=w_send.at[d],
            recv_sem=w_recv.at[d],
            device_id=device(position, source),
            device_id_type=MESH,
        )

    def x_copy(slot, d, source, target):
        span_heads = pl.ds(slot * group, sized(slot))
        return pltpu.make_async_remote_copy(
            src_ref=o_all.at[source, span_heads],
            dst_ref=o_all.at[source, span_heads],
            send_sem=x_send.at[slot, d],
            recv_sem=x_recv.at[slot, d],
            device_id=device(position, target),
            device_id_type=MESH,
        )

    def halo_frames(d):
        return min(span, halo - span * (d - 1))

    def halo_copy(slot, d, upward, arriving):
        n = halo_frames(d)
        if upward:
            src_frame, dst_frame = halo + span - n, span - n - span * d + halo
        else:
            src_frame, dst_frame = halo, halo + span * d
        which = 2 * (d - 1) + (0 if upward else 1)
        away = d * group if upward != arriving else -d * group
        return pltpu.make_async_remote_copy(
            src_ref=kv_all[slot].at[:, pl.ds(src_frame, n)],
            dst_ref=kv_all[slot].at[:, pl.ds(dst_frame, n)],
            send_sem=halo_send.at[slot, which],
            recv_sem=halo_recv.at[slot, which],
            device_id=device(position + away, tp),
            device_id_type=MESH,
        )

    def exists(d, up):
        return plane + d < groups if up else plane - d >= 0

    have = [head_of(member, slot) < heads for slot in range(slots)]

    for slot in range(slots):
        span_heads = range(slot * group, slot * group + sized(slot))
        for head in span_heads:
            for f in range(own_frames):
                part = slice(f * FRAME, (f + 1) * FRAME)
                kv_own[head, 0, f] = rotated(k_ref, f, head)
                kv_own[head, 1, f] = v_ref[
                    part, head * HEAD_DIM : (head + 1) * HEAD_DIM
                ]
        for d in range(1, group):
            target = to_member(d)

            @pl.when(head_of(target, slot) < heads)
            def _():
                kv_copy(slot, d, member, target).start()

        for head in span_heads:
            for f in range(own_frames):
                part = slice(f * FRAME, (f + 1) * FRAME)
                q_own[head, part, :] = rotated(q_ref, f, head)
        for d in range(1, group):
            target = to_member(d)

            @pl.when(head_of(target, slot) < heads)
            def _():
                q_copy(slot, d, member, target).start()

    own_weight = pltpu.make_async_copy(
        w_ref.at[:, pl.ds(pl.multiple_of(tp * columns, columns), columns)],
        w_all.at[tp],
        w_local,
    )
    own_weight.start()
    for d in range(1, peers):
        w_copy(d).start()

    for slot in range(slots):

        @pl.when(have[slot])
        def _():
            mine = head_of(member, slot)
            kv_all[slot][:, own_rows(member)] = kv_own[mine]
            q_all[slot, query_rows(member), :] = q_own[mine]

            for d in range(1, reach + 1):
                for up in (True, False):

                    @pl.when(jnp.logical_not(exists(d, up)))
                    def _():
                        n = halo_frames(d)
                        blank = halo + span * d if up else span - n - span * d + halo
                        kv_all[slot][:, blank : blank + n] = jnp.zeros(
                            (2, n, FRAME, HEAD_DIM), jnp.bfloat16
                        )

            for d in range(1, group):
                kv_copy(slot, d, from_member(d), member).wait_recv()
            for d in range(1, reach + 1):
                for up in (True, False):

                    @pl.when(exists(d, up))
                    def _():
                        halo_copy(slot, d, up, False).start()

    scale = HEAD_DIM**-0.5 * math.log2(math.e)
    window = longest * FRAME
    column = lax.broadcasted_iota(jnp.int32, (1, window), 1)

    for slot in range(slots):

        @pl.when(have[slot])
        def _():
            mine = head_of(member, slot)
            for d in range(1, group):
                q_copy(slot, d, from_member(d), member).wait_recv()
            for d in range(1, reach + 1):
                for up in (True, False):

                    @pl.when(exists(d, not up))
                    def _():
                        halo_copy(slot, d, up, True).wait_recv()

            def attend(step, carry):
                d = lax.rem(step + 1, group)
                target = to_member(d)
                for f in range(own_frames):
                    place = target * own_frames + f
                    start, stop = clip_span(counts_ref, clips, longest, first_frame + place)
                    here = pl.ds(pl.multiple_of(place * FRAME, FRAME), FRAME)
                    first_key = start - first_frame + halo
                    keys = jnp.concatenate(
                        [kv_all[slot][0, first_key + i] for i in range(longest)], axis=0
                    )
                    values = jnp.concatenate(
                        [kv_all[slot][1, first_key + i] for i in range(longest)], axis=0
                    )
                    scores = lax.dot_general(
                        q_all[slot, here, :],
                        keys,
                        (((1,), (1,)), ((), ())),
                        preferred_element_type=jnp.float32,
                    )
                    scores = jnp.where(column < (stop - start) * FRAME, scores, NEG_FILL)
                    largest = jnp.max(scores, axis=1, keepdims=True)
                    expo = jnp.exp2((scores - largest) * scale)
                    total = jnp.sum(expo, axis=1, keepdims=True)
                    summed = jnp.dot(
                        expo.astype(jnp.bfloat16), values, preferred_element_type=jnp.float32
                    )
                    o_mine[slot, here, :] = (summed / total).astype(jnp.bfloat16)

                @pl.when(d > 0)
                def _():
                    o_copy(slot, d, member, target).start()

                return carry

            lax.fori_loop(0, group, attend, 0)
            o_all[tp, mine] = o_mine[slot, query_rows(member), :]

    for slot in range(slots):
        for d in range(1, group):
            source = from_member(d)

            @pl.when(head_of(source, slot) < heads)
            def _():
                o_copy(slot, d, source, member).wait_recv()

        for d in range(1, peers):
            x_copy(slot, d, tp, lax.rem(tp + d, peers)).start()

    chunk = 256
    own_weight.wait()

    def project(source, into, last):
        left = jnp.concatenate([o_all[source, head] for head in range(heads)], axis=1)

        def body(step, carry):
            place = pl.ds(pl.multiple_of(step * chunk, chunk), chunk)
            term = jnp.dot(left, w_all[source, :, place], preferred_element_type=jnp.float32)
            if into:
                term = total_ref[:, place] + term
            if last:
                out_ref[:, place] = term.astype(jnp.bfloat16)
            else:
                total_ref[:, place] = term
            return carry

        lax.fori_loop(0, columns // chunk, body, 0)

    project(tp, False, peers == 1)
    for d in range(1, peers):
        source = lax.rem(tp - d + peers, peers)
        w_arrival(d).wait_recv()
        for slot in range(slots):
            x_copy(slot, d, source, tp).wait_recv()
        project(source, True, d == peers - 1)

    for d in range(1, peers):
        w_copy(d).wait_send()
    for slot in range(slots):
        for d in range(1, peers):
            x_copy(slot, d, tp, lax.rem(tp + d, peers)).wait_send()
        for d in range(1, group):
            target = to_member(d)

            @pl.when(head_of(target, slot) < heads)
            def _():
                kv_copy(slot, d, member, target).wait_send()
                q_copy(slot, d, member, target).wait_send()

            @pl.when(have[slot])
            def _():
                o_copy(slot, d, member, target).wait_send()

        for d in range(1, reach + 1):
            for up in (True, False):

                @pl.when(have[slot] & exists(d, up))
                def _():
                    halo_copy(slot, d, up, False).wait_send()


def per_device(seq, peers, query_rows, key_rows, value_rows, frame_counts, out_weight):
    rows, features = query_rows.shape
    heads = features // HEAD_DIM
    own_frames = rows // FRAME
    longest = own_frames * seq // 8
    group = 4
    groups = seq // group
    slots = -(-heads // group)
    columns = out_weight.shape[1] // peers
    clips = frame_counts.shape[0]
    span = group * own_frames
    halo = longest - 1
    reach = -(-halo // span)
    dims = (heads, group, groups, peers, slots, longest, clips, own_frames)
    vmem = pl.BlockSpec(memory_space=pltpu.VMEM)
    dma = pltpu.SemaphoreType.DMA
    bf16 = jnp.bfloat16
    flops = 2 * rows * features * out_weight.shape[1]
    return pl.pallas_call(
        functools.partial(kernel, dims),
        out_shape=jax.ShapeDtypeStruct((rows, columns), bf16),
        in_specs=[
            pl.BlockSpec(memory_space=pltpu.SMEM),
            vmem,
            vmem,
            vmem,
            pl.BlockSpec(memory_space=pl.ANY),
        ]
        + [vmem] * 5,
        out_specs=vmem,
        scratch_shapes=[
            pltpu.VMEM((heads, rows, HEAD_DIM), bf16),
            pltpu.VMEM((heads, 2, own_frames, FRAME, HEAD_DIM), bf16),
            pltpu.VMEM((slots, group * rows, HEAD_DIM), bf16),
            [pltpu.VMEM((2, span + 2 * halo, FRAME, HEAD_DIM), bf16)] * slots,
            pltpu.VMEM((slots, group * rows, HEAD_DIM), bf16),
            pltpu.VMEM((peers, heads, rows, HEAD_DIM), bf16),
            pltpu.VMEM((peers, features, columns), bf16),
            pltpu.VMEM((rows, columns), jnp.float32),
            dma(()),
            dma((peers,)),
            dma((peers,)),
            dma((slots, group)),
            dma((slots, group)),
            dma((slots, group)),
            dma((slots, group)),
            dma((slots, 2 * reach)),
            dma((slots, 2 * reach)),
            dma((slots, group)),
            dma((slots, group)),
            dma((slots, peers)),
            dma((slots, peers)),
        ],
        compiler_params=pltpu.CompilerParams(
            collective_id=0, has_side_effects=True, vmem_limit_bytes=56 * 1024 * 1024
        ),
        cost_estimate=pl.CostEstimate(flops=flops, bytes_accessed=8 << 20, transcendentals=0),
    )(frame_counts, query_rows, key_rows, value_rows, out_weight, *rope_tables(longest))


def solution(mesh):
    return jax.shard_map(
        functools.partial(per_device, mesh.shape["seq"], mesh.shape["tp"]),
        mesh=mesh,
        in_specs=(P("seq", "tp"), P("seq", "tp"), P("seq", "tp"), P(), P("tp", None)),
        out_specs=P("seq", "tp"),
        check_vma=False,
    )
```

```python
import functools
import math

import jax
import jax.numpy as jnp
import numpy as np
from jax import lax
from jax.experimental import pallas as pl
from jax.experimental.pallas import tpu as pltpu
from jax.sharding import PartitionSpec as P

SECTIONS = (16, 56, 56)
PH = 16
PW = 16
FRAME = PH * PW
HEAD_DIM = 128
ROPE_BASE = 256.0
NEG_FILL = -1e30
MESH = pl.DeviceIdType.MESH


def rope_tables(longest):
    angle_hw = np.zeros((FRAME, HEAD_DIM), np.float64)
    angle_t = np.zeros((longest, HEAD_DIM), np.float64)
    pairing = np.zeros((HEAD_DIM, HEAD_DIM), np.float32)
    row = np.arange(FRAME)
    first = 0
    for section, width in enumerate(SECTIONS):
        half = width // 2
        frequency = np.exp(-(2.0 * np.arange(half) / width) * math.log(ROPE_BASE))
        frequency = np.concatenate([frequency, frequency])
        lanes = slice(first, first + width)
        if section == 0:
            angle_t[:, lanes] = np.arange(longest)[:, None] * frequency[None, :]
        else:
            place = row // PW if section == 1 else row % PW
            angle_hw[:, lanes] = place[:, None] * frequency[None, :]
        for j in range(half):
            pairing[first + half + j, first + j] = -1.0
            pairing[first + j, first + half + j] = 1.0
        first += width
    angle_t = angle_t[:, None, :]
    tables = [np.cos(angle_hw), np.sin(angle_hw), np.cos(angle_t), np.sin(angle_t)]
    return [jnp.asarray(table, jnp.float32) for table in tables] + [
        jnp.asarray(pairing, jnp.bfloat16)
    ]


def clip_span(counts_ref, clips, longest, frame):
    start = jnp.int32(0)
    stop = jnp.int32(1 << 30)
    end = jnp.int32(0)
    for clip in range(clips):
        end = end + counts_ref[clip]
        start = jnp.where(end <= frame, end, start)
        stop = jnp.where(end > frame, jnp.minimum(stop, end), stop)
    return jnp.clip(start, frame - (longest - 1), frame), stop


def kernel(
    dims,
    counts_ref,
    q_ref,
    k_ref,
    v_ref,
    w_ref,
    cos_hw,
    sin_hw,
    cos_t,
    sin_t,
    pairing,
    out_ref,
    q_in,
    k_in,
    q_own,
    k_own,
    q_all,
    k_all,
    v_all,
    o_mine,
    o_all,
    w_all,
    total_ref,
    in_local,
    w_local,
    v_local,
    w_send,
    w_recv,
    k_send,
    k_recv,
    v_send,
    v_recv,
    q_send,
    q_recv,
    halo_send,
    halo_recv,
    o_send,
    o_recv,
    x_send,
    x_recv,
):
    heads, group, groups, peers, slots, longest, clips, own_frames = dims
    rows = own_frames * FRAME
    halo = longest - 1
    span = group * own_frames
    reach = (halo + span - 1) // span
    columns = out_ref.shape[1]
    position = lax.axis_index("seq")
    tp = lax.axis_index("tp")
    plane = position // group
    member = position % group
    first_frame = plane * span

    def head_of(who, slot):
        return lax.rem(who - 2 * tp + 2 * group * peers, group) + slot * group

    def sized(slot):
        return min(group, heads - slot * group)

    def to_member(d):
        return lax.rem(member + d, group)

    def from_member(d):
        return lax.rem(member - d + group, group)

    def device(seq, core):
        return (seq, core)

    loads = [
        pltpu.make_async_copy(k_ref, k_in, in_local.at[0]),
        pltpu.make_async_copy(q_ref, q_in, in_local.at[1]),
    ]
    for load in loads:
        load.start()

    barrier = pltpu.get_barrier_semaphore()
    for d in range(1, group):
        pl.semaphore_signal(
            barrier, inc=1, device_id=device(plane * group + to_member(d), tp), device_id_type=MESH
        )
    for d in range(1, peers):
        pl.semaphore_signal(
            barrier, inc=1, device_id=device(position, lax.rem(tp + d, peers)), device_id_type=MESH
        )
    greeted = jnp.int32(group - 1 + peers - 1)
    for d in range(1, reach + 1):
        above = plane + d < groups
        below = plane - d >= 0

        @pl.when(above)
        def _():
            pl.semaphore_signal(
                barrier, inc=1, device_id=device(position + d * group, tp), device_id_type=MESH
            )

        @pl.when(below)
        def _():
            pl.semaphore_signal(
                barrier, inc=1, device_id=device(position - d * group, tp), device_id_type=MESH
            )

        greeted = greeted + above.astype(jnp.int32) + below.astype(jnp.int32)
    pl.semaphore_wait(barrier, greeted)

    lane = lax.broadcasted_iota(jnp.int32, (FRAME, HEAD_DIM), 1)
    in_t = lane < SECTIONS[0]
    cosines, sines = [], []
    for f in range(own_frames):
        frame = position * own_frames + f
        t = frame - clip_span(counts_ref, clips, longest, frame)[0]
        cosines.append(jnp.where(in_t, cos_t[t], cos_hw[...]))
        sines.append(jnp.where(in_t, sin_t[t], sin_hw[...]))

    def rotated(ref, f, head):
        x = ref[f * FRAME : (f + 1) * FRAME, head * HEAD_DIM : (head + 1) * HEAD_DIM]
        paired = jnp.dot(x, pairing[...], preferred_element_type=jnp.float32)
        return (x.astype(jnp.float32) * cosines[f] + paired * sines[f]).astype(jnp.bfloat16)

    def own_rows(who):
        return pl.ds(halo + who * own_frames, own_frames)

    def query_rows(who):
        return pl.ds(pl.multiple_of(who * rows, rows), rows)

    def lanes_of(head):
        return pl.ds(pl.multiple_of(head * HEAD_DIM, HEAD_DIM), HEAD_DIM)

    def k_copy(slot, d, source, target):
        return pltpu.make_async_remote_copy(
            src_ref=k_own.at[head_of(target, slot)],
            dst_ref=k_all[slot].at[own_rows(source)],
            send_sem=k_send.at[slot, d],
            recv_sem=k_recv.at[slot, d],
            device_id=device(plane * group + target, tp),
            device_id_type=MESH,
        )

    def v_copy(slot, d, source, target):
        return pltpu.make_async_remote_copy(
            src_ref=v_ref.at[:, :, lanes_of(head_of(target, slot))],
            dst_ref=v_all[slot].at[own_rows(source)],
            send_sem=v_send.at[slot, d],
            recv_sem=v_recv.at[slot, d],
            device_id=device(plane * group + target, tp),
            device_id_type=MESH,
        )

    def v_stay(slot):
        return pltpu.make_async_copy(
            v_ref.at[:, :, lanes_of(head_of(member, slot))],
            v_all[slot].at[own_rows(member)],
            v_local.at[slot],
        )

    def q_copy(slot, d, source, target):
        return pltpu.make_async_remote_copy(
            src_ref=q_own.at[head_of(target, slot)],
            dst_ref=q_all.at[slot, query_rows(source), :],
            send_sem=q_send.at[slot, d],
            recv_sem=q_recv.at[slot, d],
            device_id=device(plane * group + target, tp),
            device_id_type=MESH,
        )

    def o_copy(slot, d, source, target):
        return pltpu.make_async_remote_copy(
            src_ref=o_mine.at[slot, query_rows(target), :],
            dst_ref=o_all.at[tp, head_of(source, slot)],
            send_sem=o_send.at[slot, d],
            recv_sem=o_recv.at[slot, d],
            device_id=device(plane * group + target, tp),
            device_id_type=MESH,
        )

    def w_copy(d):
        target = lax.rem(tp + d, peers)
        return pltpu.make_async_remote_copy(
            src_ref=w_ref.at[:, pl.ds(pl.multiple_of(target * columns, columns), columns)],
            dst_ref=w_all.at[tp],
            send_sem=w_send.at[d],
            recv_sem=w_recv.at[d],
            device_id=device(position, target),
            device_id_type=MESH,
        )

    def w_arrival(d):
        source = lax.rem(tp - d + peers, peers)
        return pltpu.make_async_remote_copy(
            src_ref=w_ref.at[:, pl.ds(pl.multiple_of(tp * columns, columns), columns)],
            dst_ref=w_all.at[source],
            send_sem=w_send.at[d],
            recv_sem=w_recv.at[d],
            device_id=device(position, source),
            device_id_type=MESH,
        )

    def x_copy(slot, d, source, target):
        span_heads = pl.ds(slot * group, sized(slot))
        return pltpu.make_async_remote_copy(
            src_ref=o_all.at[source, span_heads],
            dst_ref=o_all.at[source, span_heads],
            send_sem=x_send.at[slot, d],
            recv_sem=x_recv.at[slot, d],
            device_id=device(position, target),
            device_id_type=MESH,
        )

    def halo_frames(d):
        return min(span, halo - span * (d - 1))

    def halo_copy(slot, what, d, upward, arriving):
        n = halo_frames(d)
        if upward:
            src_frame, dst_frame = halo + span - n, span - n - span * d + halo
        else:
            src_frame, dst_frame = halo, halo + span * d
        which = 2 * (d - 1) + (0 if upward else 1)
        away = d * group if upward != arriving else -d * group
        buffer = (k_all, v_all)[what][slot]
        return pltpu.make_async_remote_copy(
            src_ref=buffer.at[pl.ds(src_frame, n)],
            dst_ref=buffer.at[pl.ds(dst_frame, n)],
            send_sem=halo_send.at[slot, what, which],
            recv_sem=halo_recv.at[slot, what, which],
            device_id=device(position + away, tp),
            device_id_type=MESH,
        )

    def exists(d, up):
        return plane + d < groups if up else plane - d >= 0

    have = [head_of(member, slot) < heads for slot in range(slots)]

    def send(copy, slot):
        for d in range(1, group):
            target = to_member(d)

            @pl.when(head_of(target, slot) < heads)
            def _():
                copy(slot, d, member, target).start()

    own_weight = pltpu.make_async_copy(
        w_ref.at[:, pl.ds(pl.multiple_of(tp * columns, columns), columns)],
        w_all.at[tp],
        w_local,
    )

    for slot in range(slots):
        slot_heads = range(slot * group, slot * group + sized(slot))
        send(v_copy, slot)

        @pl.when(have[slot])
        def _():
            v_stay(slot).start()

        if slot == 0:
            loads[0].wait()
        for head in slot_heads:
            for f in range(own_frames):
                k_own[head, f] = rotated(k_in, f, head)
        send(k_copy, slot)
        if slot == 0:
            loads[1].wait()
        for head in slot_heads:
            for f in range(own_frames):
                part = slice(f * FRAME, (f + 1) * FRAME)
                q_own[head, part, :] = rotated(q_in, f, head)
        send(q_copy, slot)
        if slot == 0:
            own_weight.start()
            for d in range(1, peers):
                w_copy(d).start()

    scale = HEAD_DIM**-0.5 * math.log2(math.e)

    def start_halos(slot, what):
        for d in range(1, reach + 1):
            for up in (True, False):

                @pl.when(exists(d, up))
                def _():
                    halo_copy(slot, what, d, up, False).start()

    def spread(slot):
        mine = head_of(member, slot)
        k_all[slot][own_rows(member)] = k_own[mine]
        q_all[slot, query_rows(member), :] = q_own[mine]
        for d in range(1, reach + 1):
            for up in (True, False):

                @pl.when(jnp.logical_not(exists(d, up)))
                def _():
                    n = halo_frames(d)
                    blank = halo + span * d if up else span - n - span * d + halo
                    for buffer in (k_all, v_all):
                        buffer[slot][blank : blank + n] = jnp.zeros(
                            (n, FRAME, HEAD_DIM), jnp.bfloat16
                        )

        v_stay(slot).wait()
        for d in range(1, group):
            v_copy(slot, d, from_member(d), member).wait_recv()
        start_halos(slot, 1)
        for d in range(1, group):
            k_copy(slot, d, from_member(d), member).wait_recv()
        start_halos(slot, 0)

    def settle(slot):
        for d in range(1, group):
            q_copy(slot, d, from_member(d), member).wait_recv()
        for what in (1, 0):
            for d in range(1, reach + 1):
                for up in (True, False):

                    @pl.when(exists(d, not up))
                    def _():
                        halo_copy(slot, what, d, up, True).wait_recv()

    ones = jnp.ones((FRAME, HEAD_DIM), jnp.bfloat16)

    def attend(slot, step, carry):
        d = lax.rem(step + 1, group)
        target = to_member(d)
        for f in range(own_frames):
            place = target * own_frames + f
            start, stop = clip_span(counts_ref, clips, longest, first_frame + place)
            here = pl.ds(pl.multiple_of(place * FRAME, FRAME), FRAME)
            first_key = start - first_frame + halo
            queries = q_all[slot, here, :]
            scores, tops, values, inside = [], [], [], []
            largest = None
            for i in range(longest):
                part = lax.dot_general(
                    queries,
                    k_all[slot][first_key + i],
                    (((1,), (1,)), ((), ())),
                    preferred_element_type=jnp.float32,
                )
                top = jnp.max(part, axis=1, keepdims=True)
                same = jnp.full((FRAME, 1), start + i, jnp.int32) < stop
                kept = jnp.where(same, top, NEG_FILL)
                largest = kept if i == 0 else jnp.maximum(largest, kept)
                both = jnp.concatenate([v_all[slot][first_key + i], ones], axis=1)
                in_clip = jnp.full(both.shape, start + i, jnp.int32) < stop
                scores.append(part)
                tops.append(top)
                inside.append(same)
                values.append(jnp.where(in_clip, both, jnp.zeros_like(both)))
            weights = [
                jnp.exp2((part - jnp.where(same, largest, top)) * scale).astype(jnp.bfloat16)
                for part, same, top in zip(scores, inside, tops)
            ]
            summed = jnp.dot(
                jnp.concatenate(weights, axis=1),
                jnp.concatenate(values, axis=0),
                preferred_element_type=jnp.float32,
            )
            o_mine[slot, here, :] = (
                summed[:, :HEAD_DIM] / summed[:, HEAD_DIM:]
            ).astype(jnp.bfloat16)

        @pl.when(d > 0)
        def _():
            o_copy(slot, d, member, target).start()

        return carry

    @pl.when(have[0])
    def _():
        spread(0)
        settle(0)
        lax.fori_loop(0, group // 2, functools.partial(attend, 0), 0)

    for slot in range(1, slots + 1):
        if slot < slots:

            @pl.when(have[slot])
            def _():
                spread(slot)

        @pl.when(have[slot - 1])
        def _():
            lax.fori_loop(group // 2, group, functools.partial(attend, slot - 1), 0)
            o_all[tp, head_of(member, slot - 1)] = o_mine[slot - 1, query_rows(member), :]

        if slot < slots:

            @pl.when(have[slot])
            def _():
                settle(slot)
                lax.fori_loop(0, group // 2, functools.partial(attend, slot), 0)

    chunk = 256

    def project(source, slot, first, last):
        slot_heads = range(slot * group, slot * group + sized(slot))
        left = jnp.concatenate([o_all[source, head] for head in slot_heads], axis=1)
        deep = slice(slot * group * HEAD_DIM, (slot * group + sized(slot)) * HEAD_DIM)

        def body(step, carry):
            place = pl.ds(pl.multiple_of(step * chunk, chunk), chunk)
            term = jnp.dot(left, w_all[source, deep, place], preferred_element_type=jnp.float32)
            if not first:
                term = total_ref[:, place] + term
            if last:
                out_ref[:, place] = term.astype(jnp.bfloat16)
            else:
                total_ref[:, place] = term
            return carry

        lax.fori_loop(0, columns // chunk, body, 0)

    own_weight.wait()
    for slot in range(slots):
        for d in range(1, group):
            source = from_member(d)

            @pl.when(head_of(source, slot) < heads)
            def _():
                o_copy(slot, d, source, member).wait_recv()

        for d in range(1, peers):
            x_copy(slot, d, tp, lax.rem(tp + d, peers)).start()
        project(tp, slot, slot == 0, peers == 1 and slot == slots - 1)

    for d in range(1, peers):
        w_arrival(d).wait_recv()
    for slot in range(slots):
        for d in range(1, peers):
            source = lax.rem(tp - d + peers, peers)
            x_copy(slot, d, source, tp).wait_recv()
            project(source, slot, False, slot == slots - 1 and d == peers - 1)

    for d in range(1, peers):
        w_copy(d).wait_send()
    for slot in range(slots):
        for d in range(1, peers):
            x_copy(slot, d, tp, lax.rem(tp + d, peers)).wait_send()
        for d in range(1, group):
            target = to_member(d)

            @pl.when(head_of(target, slot) < heads)
            def _():
                k_copy(slot, d, member, target).wait_send()
                v_copy(slot, d, member, target).wait_send()
                q_copy(slot, d, member, target).wait_send()

            @pl.when(have[slot])
            def _():
                o_copy(slot, d, member, target).wait_send()

        for d in range(1, reach + 1):
            for up in (True, False):

                @pl.when(have[slot] & exists(d, up))
                def _():
                    for what in (0, 1):
                        halo_copy(slot, what, d, up, False).wait_send()


def per_device(seq, peers, query_rows, key_rows, value_rows, frame_counts, out_weight):
    rows, features = query_rows.shape
    heads = features // HEAD_DIM
    own_frames = rows // FRAME
    longest = own_frames * seq // 8
    group = 4
    groups = seq // group
    slots = -(-heads // group)
    columns = out_weight.shape[1] // peers
    clips = frame_counts.shape[0]
    span = group * own_frames
    halo = longest - 1
    reach = -(-halo // span)
    dims = (heads, group, groups, peers, slots, longest, clips, own_frames)
    value_frames = value_rows.reshape(own_frames, FRAME, features)
    vmem = pl.BlockSpec(memory_space=pltpu.VMEM)
    dma = pltpu.SemaphoreType.DMA
    bf16 = jnp.bfloat16
    flops = 2 * rows * features * out_weight.shape[1]
    return pl.pallas_call(
        functools.partial(kernel, dims),
        out_shape=jax.ShapeDtypeStruct((rows, columns), bf16),
        in_specs=[
            pl.BlockSpec(memory_space=pltpu.SMEM),
        ]
        + [pl.BlockSpec(memory_space=pl.ANY)] * 4
        + [vmem] * 5,
        out_specs=vmem,
        scratch_shapes=[
            pltpu.VMEM((rows, features), bf16),
            pltpu.VMEM((rows, features), bf16),
            pltpu.VMEM((heads, rows, HEAD_DIM), bf16),
            pltpu.VMEM((heads, own_frames, FRAME, HEAD_DIM), bf16),
            pltpu.VMEM((slots, group * rows, HEAD_DIM), bf16),
            [pltpu.VMEM((span + 2 * halo, FRAME, HEAD_DIM), bf16)] * slots,
            [pltpu.VMEM((span + 2 * halo, FRAME, HEAD_DIM), bf16)] * slots,
            pltpu.VMEM((slots, group * rows, HEAD_DIM), bf16),
            pltpu.VMEM((peers, heads, rows, HEAD_DIM), bf16),
            pltpu.VMEM((peers, features, columns), bf16),
            pltpu.VMEM((rows, columns), jnp.float32),
            dma((2,)),
            dma(()),
            dma((slots,)),
            dma((peers,)),
            dma((peers,)),
            dma((slots, group)),
            dma((slots, group)),
            dma((slots, group)),
            dma((slots, group)),
            dma((slots, group)),
            dma((slots, group)),
            dma((slots, 2, 2 * reach)),
            dma((slots, 2, 2 * reach)),
            dma((slots, group)),
            dma((slots, group)),
            dma((slots, peers)),
            dma((slots, peers)),
        ],
        compiler_params=pltpu.CompilerParams(
            collective_id=0, has_side_effects=True, vmem_limit_bytes=56 * 1024 * 1024
        ),
        cost_estimate=pl.CostEstimate(flops=flops, bytes_accessed=8 << 20, transcendentals=0),
    )(frame_counts, query_rows, key_rows, value_frames, out_weight, *rope_tables(longest))


def solution(mesh):
    return jax.shard_map(
        functools.partial(per_device, mesh.shape["seq"], mesh.shape["tp"]),
        mesh=mesh,
        in_specs=(P("seq", "tp"), P("seq", "tp"), P("seq", "tp"), P(), P("tp", None)),
        out_specs=P("seq", "tp"),
        check_vma=False,
    )
```

```python
import functools
import math

import jax
import jax.numpy as jnp
import numpy as np
from jax import lax
from jax.experimental import pallas as pl
from jax.experimental.pallas import tpu as pltpu
from jax.sharding import PartitionSpec as P

SECTIONS = (16, 56, 56)
PH = 16
PW = 16
FRAME = PH * PW
HEAD_DIM = 128
ROPE_BASE = 256.0
NEG_FILL = -1e30
MESH = pl.DeviceIdType.MESH


def rope_tables(longest):
    angle_hw = np.zeros((FRAME, HEAD_DIM), np.float64)
    angle_t = np.zeros((longest, HEAD_DIM), np.float64)
    pairing = np.zeros((HEAD_DIM, HEAD_DIM), np.float32)
    row = np.arange(FRAME)
    first = 0
    for section, width in enumerate(SECTIONS):
        half = width // 2
        frequency = np.exp(-(2.0 * np.arange(half) / width) * math.log(ROPE_BASE))
        frequency = np.concatenate([frequency, frequency])
        lanes = slice(first, first + width)
        if section == 0:
            angle_t[:, lanes] = np.arange(longest)[:, None] * frequency[None, :]
        else:
            place = row // PW if section == 1 else row % PW
            angle_hw[:, lanes] = place[:, None] * frequency[None, :]
        for j in range(half):
            pairing[first + half + j, first + j] = -1.0
            pairing[first + j, first + half + j] = 1.0
        first += width
    angle_t = angle_t[:, None, :]
    tables = [np.cos(angle_hw), np.sin(angle_hw), np.cos(angle_t), np.sin(angle_t)]
    return [jnp.asarray(table, jnp.float32) for table in tables] + [
        jnp.asarray(pairing, jnp.bfloat16)
    ]


def clip_span(counts_ref, clips, longest, frame):
    start = jnp.int32(0)
    stop = jnp.int32(1 << 30)
    end = jnp.int32(0)
    for clip in range(clips):
        end = end + counts_ref[clip]
        start = jnp.where(end <= frame, end, start)
        stop = jnp.where(end > frame, jnp.minimum(stop, end), stop)
    return jnp.clip(start, frame - (longest - 1), frame), stop


def kernel(
    dims,
    counts_ref,
    q_ref,
    k_ref,
    v_ref,
    w_ref,
    cos_hw_ref,
    sin_hw_ref,
    cos_t_ref,
    sin_t_ref,
    pairing_ref,
    out_ref,
    q_in,
    k_in,
    cos_hw,
    sin_hw,
    cos_t,
    sin_t,
    pairing,
    q_own,
    k_own,
    q_all,
    k_all,
    v_all,
    o_mine,
    o_all,
    w_all,
    total_ref,
    in_local,
    w_local,
    v_local,
    w_send,
    w_recv,
    k_send,
    k_recv,
    v_send,
    v_recv,
    q_send,
    q_recv,
    halo_send,
    halo_recv,
    o_send,
    o_recv,
    x_send,
    x_recv,
):
    heads, group, groups, peers, slots, longest, clips, own_frames = dims
    rows = own_frames * FRAME
    halo = longest - 1
    span = group * own_frames
    reach = (halo + span - 1) // span
    columns = out_ref.shape[1]
    position = lax.axis_index("seq")
    tp = lax.axis_index("tp")
    plane = position // group
    member = position % group
    first_frame = plane * span

    def head_of(who, slot):
        return lax.rem(who - 2 * tp + 2 * group * peers, group) + slot * group

    def sized(slot):
        return min(group, heads - slot * group)

    def to_member(d):
        return lax.rem(member + d, group)

    def from_member(d):
        return lax.rem(member - d + group, group)

    def device(seq, core):
        return (seq, core)

    loads = [
        pltpu.make_async_copy(source, target, in_local.at[i])
        for i, (source, target) in enumerate(
            [
                (cos_hw_ref, cos_hw),
                (sin_hw_ref, sin_hw),
                (cos_t_ref, cos_t),
                (sin_t_ref, sin_t),
                (pairing_ref, pairing),
                (k_ref, k_in),
                (q_ref, q_in),
            ]
        )
    ]
    for load in loads:
        load.start()

    barrier = pltpu.get_barrier_semaphore()
    for d in range(1, group):
        pl.semaphore_signal(
            barrier, inc=1, device_id=device(plane * group + to_member(d), tp), device_id_type=MESH
        )
    for d in range(1, peers):
        pl.semaphore_signal(
            barrier, inc=1, device_id=device(position, lax.rem(tp + d, peers)), device_id_type=MESH
        )
    greeted = jnp.int32(group - 1 + peers - 1)
    for d in range(1, reach + 1):
        above = plane + d < groups
        below = plane - d >= 0

        @pl.when(above)
        def _():
            pl.semaphore_signal(
                barrier, inc=1, device_id=device(position + d * group, tp), device_id_type=MESH
            )

        @pl.when(below)
        def _():
            pl.semaphore_signal(
                barrier, inc=1, device_id=device(position - d * group, tp), device_id_type=MESH
            )

        greeted = greeted + above.astype(jnp.int32) + below.astype(jnp.int32)
    pl.semaphore_wait(barrier, greeted)

    cosines, sines = [], []

    def rotated(ref, f, head):
        x = ref[f * FRAME : (f + 1) * FRAME, head * HEAD_DIM : (head + 1) * HEAD_DIM]
        paired = jnp.dot(x, pairing[...], preferred_element_type=jnp.float32)
        return (x.astype(jnp.float32) * cosines[f] + paired * sines[f]).astype(jnp.bfloat16)

    def own_rows(who):
        return pl.ds(halo + who * own_frames, own_frames)

    def query_rows(who):
        return pl.ds(pl.multiple_of(who * rows, rows), rows)

    def lanes_of(head):
        return pl.ds(pl.multiple_of(head * HEAD_DIM, HEAD_DIM), HEAD_DIM)

    def k_copy(slot, d, source, target):
        return pltpu.make_async_remote_copy(
            src_ref=k_own.at[head_of(target, slot)],
            dst_ref=k_all[slot].at[own_rows(source)],
            send_sem=k_send.at[slot, d],
            recv_sem=k_recv.at[slot, d],
            device_id=device(plane * group + target, tp),
            device_id_type=MESH,
        )

    def v_copy(slot, d, source, target):
        return pltpu.make_async_remote_copy(
            src_ref=v_ref.at[:, :, lanes_of(head_of(target, slot))],
            dst_ref=v_all[slot].at[own_rows(source)],
            send_sem=v_send.at[slot, d],
            recv_sem=v_recv.at[slot, d],
            device_id=device(plane * group + target, tp),
            device_id_type=MESH,
        )

    def v_stay(slot):
        return pltpu.make_async_copy(
            v_ref.at[:, :, lanes_of(head_of(member, slot))],
            v_all[slot].at[own_rows(member)],
            v_local.at[slot],
        )

    def q_copy(slot, d, source, target):
        return pltpu.make_async_remote_copy(
            src_ref=q_own.at[head_of(target, slot)],
            dst_ref=q_all.at[slot, query_rows(source), :],
            send_sem=q_send.at[slot, d],
            recv_sem=q_recv.at[slot, d],
            device_id=device(plane * group + target, tp),
            device_id_type=MESH,
        )

    def o_copy(slot, d, source, target):
        return pltpu.make_async_remote_copy(
            src_ref=o_mine.at[slot, query_rows(target), :],
            dst_ref=o_all.at[tp, head_of(source, slot)],
            send_sem=o_send.at[slot, d],
            recv_sem=o_recv.at[slot, d],
            device_id=device(plane * group + target, tp),
            device_id_type=MESH,
        )

    def w_copy(d):
        target = lax.rem(tp + d, peers)
        return pltpu.make_async_remote_copy(
            src_ref=w_ref.at[:, pl.ds(pl.multiple_of(target * columns, columns), columns)],
            dst_ref=w_all.at[tp],
            send_sem=w_send.at[d],
            recv_sem=w_recv.at[d],
            device_id=device(position, target),
            device_id_type=MESH,
        )

    def w_arrival(d):
        source = lax.rem(tp - d + peers, peers)
        return pltpu.make_async_remote_copy(
            src_ref=w_ref.at[:, pl.ds(pl.multiple_of(tp * columns, columns), columns)],
            dst_ref=w_all.at[source],
            send_sem=w_send.at[d],
            recv_sem=w_recv.at[d],
            device_id=device(position, source),
            device_id_type=MESH,
        )

    def x_copy(slot, d, source, target):
        span_heads = pl.ds(slot * group, sized(slot))
        return pltpu.make_async_remote_copy(
            src_ref=o_all.at[source, span_heads],
            dst_ref=o_all.at[source, span_heads],
            send_sem=x_send.at[slot, d],
            recv_sem=x_recv.at[slot, d],
            device_id=device(position, target),
            device_id_type=MESH,
        )

    def halo_frames(d):
        return min(span, halo - span * (d - 1))

    def halo_copy(slot, what, d, upward, arriving):
        n = halo_frames(d)
        if upward:
            src_frame, dst_frame = halo + span - n, span - n - span * d + halo
        else:
            src_frame, dst_frame = halo, halo + span * d
        which = 2 * (d - 1) + (0 if upward else 1)
        away = d * group if upward != arriving else -d * group
        buffer = (k_all, v_all)[what][slot]
        return pltpu.make_async_remote_copy(
            src_ref=buffer.at[pl.ds(src_frame, n)],
            dst_ref=buffer.at[pl.ds(dst_frame, n)],
            send_sem=halo_send.at[slot, what, which],
            recv_sem=halo_recv.at[slot, what, which],
            device_id=device(position + away, tp),
            device_id_type=MESH,
        )

    def exists(d, up):
        return plane + d < groups if up else plane - d >= 0

    have = [head_of(member, slot) < heads for slot in range(slots)]

    def angles():
        lane = lax.broadcasted_iota(jnp.int32, (FRAME, HEAD_DIM), 1)
        in_t = lane < SECTIONS[0]
        for f in range(own_frames):
            frame = position * own_frames + f
            t = frame - clip_span(counts_ref, clips, longest, frame)[0]
            cosines.append(jnp.where(in_t, cos_t[t], cos_hw[...]))
            sines.append(jnp.where(in_t, sin_t[t], sin_hw[...]))

    def send(copy, slot):
        for d in range(1, group):
            target = to_member(d)

            @pl.when(head_of(target, slot) < heads)
            def _():
                copy(slot, d, member, target).start()

    own_weight = pltpu.make_async_copy(
        w_ref.at[:, pl.ds(pl.multiple_of(tp * columns, columns), columns)],
        w_all.at[tp],
        w_local,
    )

    for slot in range(slots):
        slot_heads = range(slot * group, slot * group + sized(slot))
        send(v_copy, slot)

        @pl.when(have[slot])
        def _():
            v_stay(slot).start()

        if slot == 0:
            for load in loads[:-1]:
                load.wait()
            angles()
        for head in slot_heads:
            for f in range(own_frames):
                k_own[head, f] = rotated(k_in, f, head)
        send(k_copy, slot)
        if slot == 0:
            loads[-1].wait()
        for head in slot_heads:
            for f in range(own_frames):
                part = slice(f * FRAME, (f + 1) * FRAME)
                q_own[head, part, :] = rotated(q_in, f, head)
        send(q_copy, slot)

    scale = HEAD_DIM**-0.5 * math.log2(math.e)

    def start_halos(slot, what):
        for d in range(1, reach + 1):
            for up in (True, False):

                @pl.when(exists(d, up))
                def _():
                    halo_copy(slot, what, d, up, False).start()

    def spread(slot):
        mine = head_of(member, slot)
        k_all[slot][own_rows(member)] = k_own[mine]
        q_all[slot, query_rows(member), :] = q_own[mine]
        for d in range(1, reach + 1):
            for up in (True, False):

                @pl.when(jnp.logical_not(exists(d, up)))
                def _():
                    n = halo_frames(d)
                    blank = halo + span * d if up else span - n - span * d + halo
                    for buffer in (k_all, v_all):
                        buffer[slot][blank : blank + n] = jnp.zeros(
                            (n, FRAME, HEAD_DIM), jnp.bfloat16
                        )

        v_stay(slot).wait()
        for d in range(1, group):
            v_copy(slot, d, from_member(d), member).wait_recv()
        start_halos(slot, 1)
        for d in range(1, group):
            k_copy(slot, d, from_member(d), member).wait_recv()
        start_halos(slot, 0)

    def settle(slot):
        for d in range(1, group):
            q_copy(slot, d, from_member(d), member).wait_recv()
        for what in (1, 0):
            for d in range(1, reach + 1):
                for up in (True, False):

                    @pl.when(exists(d, not up))
                    def _():
                        halo_copy(slot, what, d, up, True).wait_recv()

    ones = jnp.ones((FRAME, HEAD_DIM), jnp.bfloat16)

    def attend(slot, step, carry):
        d = lax.rem(step + 1, group)
        target = to_member(d)
        for f in range(own_frames):
            place = target * own_frames + f
            start, stop = clip_span(counts_ref, clips, longest, first_frame + place)
            here = pl.ds(pl.multiple_of(place * FRAME, FRAME), FRAME)
            first_key = start - first_frame + halo
            queries = q_all[slot, here, :]
            scores, tops, values, inside = [], [], [], []
            largest = None
            for i in range(longest):
                part = lax.dot_general(
                    queries,
                    k_all[slot][first_key + i],
                    (((1,), (1,)), ((), ())),
                    preferred_element_type=jnp.float32,
                )
                top = jnp.max(part, axis=1, keepdims=True)
                same = jnp.full((FRAME, 1), start + i, jnp.int32) < stop
                kept = jnp.where(same, top, NEG_FILL)
                largest = kept if i == 0 else jnp.maximum(largest, kept)
                both = jnp.concatenate([v_all[slot][first_key + i], ones], axis=1)
                in_clip = jnp.full(both.shape, start + i, jnp.int32) < stop
                scores.append(part)
                tops.append(top)
                inside.append(same)
                values.append(jnp.where(in_clip, both, jnp.zeros_like(both)))
            weights = [
                jnp.exp2((part - jnp.where(same, largest, top)) * scale).astype(jnp.bfloat16)
                for part, same, top in zip(scores, inside, tops)
            ]
            summed = jnp.dot(
                jnp.concatenate(weights, axis=1),
                jnp.concatenate(values, axis=0),
                preferred_element_type=jnp.float32,
            )
            o_mine[slot, here, :] = (
                summed[:, :HEAD_DIM] / summed[:, HEAD_DIM:]
            ).astype(jnp.bfloat16)

        @pl.when(d > 0)
        def _():
            o_copy(slot, d, member, target).start()

        return carry

    @pl.when(have[0])
    def _():
        spread(0)
        settle(0)
        lax.fori_loop(0, group // 2, functools.partial(attend, 0), 0)

    own_weight.start()
    for d in range(1, peers):
        w_copy(d).start()

    for slot in range(1, slots + 1):
        if slot < slots:

            @pl.when(have[slot])
            def _():
                spread(slot)

        @pl.when(have[slot - 1])
        def _():
            lax.fori_loop(group // 2, group, functools.partial(attend, slot - 1), 0)
            o_all[tp, head_of(member, slot - 1)] = o_mine[slot - 1, query_rows(member), :]

        if slot < slots:

            @pl.when(have[slot])
            def _():
                settle(slot)
                lax.fori_loop(0, group // 2, functools.partial(attend, slot), 0)

    chunk = 256

    def project(source, slot, first, last):
        slot_heads = range(slot * group, slot * group + sized(slot))
        left = jnp.concatenate([o_all[source, head] for head in slot_heads], axis=1)
        deep = slice(slot * group * HEAD_DIM, (slot * group + sized(slot)) * HEAD_DIM)

        def body(step, carry):
            place = pl.ds(pl.multiple_of(step * chunk, chunk), chunk)
            term = jnp.dot(left, w_all[source, deep, place], preferred_element_type=jnp.float32)
            if not first:
                term = total_ref[:, place] + term
            if last:
                out_ref[:, place] = term.astype(jnp.bfloat16)
            else:
                total_ref[:, place] = term
            return carry

        lax.fori_loop(0, columns // chunk, body, 0)

    own_weight.wait()
    for slot in range(slots):
        for d in range(1, group):
            source = from_member(d)

            @pl.when(head_of(source, slot) < heads)
            def _():
                o_copy(slot, d, source, member).wait_recv()

        for d in range(1, peers):
            x_copy(slot, d, tp, lax.rem(tp + d, peers)).start()
        project(tp, slot, slot == 0, peers == 1 and slot == slots - 1)

    for d in range(1, peers):
        w_arrival(d).wait_recv()
    for slot in range(slots):
        for d in range(1, peers):
            source = lax.rem(tp - d + peers, peers)
            x_copy(slot, d, source, tp).wait_recv()
            project(source, slot, False, slot == slots - 1 and d == peers - 1)

    for d in range(1, peers):
        w_copy(d).wait_send()
    for slot in range(slots):
        for d in range(1, peers):
            x_copy(slot, d, tp, lax.rem(tp + d, peers)).wait_send()
        for d in range(1, group):
            target = to_member(d)

            @pl.when(head_of(target, slot) < heads)
            def _():
                k_copy(slot, d, member, target).wait_send()
                v_copy(slot, d, member, target).wait_send()
                q_copy(slot, d, member, target).wait_send()

            @pl.when(have[slot])
            def _():
                o_copy(slot, d, member, target).wait_send()

        for d in range(1, reach + 1):
            for up in (True, False):

                @pl.when(have[slot] & exists(d, up))
                def _():
                    for what in (0, 1):
                        halo_copy(slot, what, d, up, False).wait_send()


def per_device(seq, peers, query_rows, key_rows, value_rows, frame_counts, out_weight):
    rows, features = query_rows.shape
    heads = features // HEAD_DIM
    own_frames = rows // FRAME
    longest = own_frames * seq // 8
    group = 4
    groups = seq // group
    slots = -(-heads // group)
    columns = out_weight.shape[1] // peers
    clips = frame_counts.shape[0]
    span = group * own_frames
    halo = longest - 1
    reach = -(-halo // span)
    dims = (heads, group, groups, peers, slots, longest, clips, own_frames)
    value_frames = value_rows.reshape(own_frames, FRAME, features)
    vmem = pl.BlockSpec(memory_space=pltpu.VMEM)
    dma = pltpu.SemaphoreType.DMA
    bf16 = jnp.bfloat16
    flops = 2 * rows * features * out_weight.shape[1]
    return pl.pallas_call(
        functools.partial(kernel, dims),
        out_shape=jax.ShapeDtypeStruct((rows, columns), bf16),
        in_specs=[
            pl.BlockSpec(memory_space=pltpu.SMEM),
        ]
        + [pl.BlockSpec(memory_space=pltpu.HBM)] * 9,
        out_specs=vmem,
        scratch_shapes=[
            pltpu.VMEM((rows, features), bf16),
            pltpu.VMEM((rows, features), bf16),
            pltpu.VMEM((FRAME, HEAD_DIM), jnp.float32),
            pltpu.VMEM((FRAME, HEAD_DIM), jnp.float32),
            pltpu.VMEM((longest, 1, HEAD_DIM), jnp.float32),
            pltpu.VMEM((longest, 1, HEAD_DIM), jnp.float32),
            pltpu.VMEM((HEAD_DIM, HEAD_DIM), bf16),
            pltpu.VMEM((heads, rows, HEAD_DIM), bf16),
            pltpu.VMEM((heads, own_frames, FRAME, HEAD_DIM), bf16),
            pltpu.VMEM((slots, group * rows, HEAD_DIM), bf16),
            [pltpu.VMEM((span + 2 * halo, FRAME, HEAD_DIM), bf16)] * slots,
            [pltpu.VMEM((span + 2 * halo, FRAME, HEAD_DIM), bf16)] * slots,
            pltpu.VMEM((slots, group * rows, HEAD_DIM), bf16),
            pltpu.VMEM((peers, heads, rows, HEAD_DIM), bf16),
            pltpu.VMEM((peers, features, columns), bf16),
            pltpu.VMEM((rows, columns), jnp.float32),
            dma((7,)),
            dma(()),
            dma((slots,)),
            dma((peers,)),
            dma((peers,)),
            dma((slots, group)),
            dma((slots, group)),
            dma((slots, group)),
            dma((slots, group)),
            dma((slots, group)),
            dma((slots, group)),
            dma((slots, 2, 2 * reach)),
            dma((slots, 2, 2 * reach)),
            dma((slots, group)),
            dma((slots, group)),
            dma((slots, peers)),
            dma((slots, peers)),
        ],
        compiler_params=pltpu.CompilerParams(
            collective_id=0, has_side_effects=True, vmem_limit_bytes=48 * 1024 * 1024
        ),
        cost_estimate=pl.CostEstimate(flops=flops, bytes_accessed=8 << 20, transcendentals=0),
    )(frame_counts, query_rows, key_rows, value_frames, out_weight, *rope_tables(longest))


def solution(mesh):
    return jax.shard_map(
        functools.partial(per_device, mesh.shape["seq"], mesh.shape["tp"]),
        mesh=mesh,
        in_specs=(P("seq", "tp"), P("seq", "tp"), P("seq", "tp"), P(), P("tp", None)),
        out_specs=P("seq", "tp"),
        check_vma=False,
    )
```

```python
import functools
import math

import jax
import jax.numpy as jnp
import numpy as np
from jax import lax
from jax.experimental import pallas as pl
from jax.experimental.pallas import tpu as pltpu
from jax.sharding import PartitionSpec as P

SECTIONS = (16, 56, 56)
PH = 16
PW = 16
FRAME = PH * PW
HEAD_DIM = 128
ROPE_BASE = 256.0
NEG_FILL = -1e30
MESH = pl.DeviceIdType.MESH


def rope_tables(longest):
    angle_hw = np.zeros((FRAME, HEAD_DIM), np.float64)
    angle_t = np.zeros((longest, HEAD_DIM), np.float64)
    pairing = np.zeros((HEAD_DIM, HEAD_DIM), np.float32)
    row = np.arange(FRAME)
    first = 0
    for section, width in enumerate(SECTIONS):
        half = width // 2
        frequency = np.exp(-(2.0 * np.arange(half) / width) * math.log(ROPE_BASE))
        frequency = np.concatenate([frequency, frequency])
        lanes = slice(first, first + width)
        if section == 0:
            angle_t[:, lanes] = np.arange(longest)[:, None] * frequency[None, :]
        else:
            place = row // PW if section == 1 else row % PW
            angle_hw[:, lanes] = place[:, None] * frequency[None, :]
        for j in range(half):
            pairing[first + half + j, first + j] = -1.0
            pairing[first + j, first + half + j] = 1.0
        first += width
    angle_t = angle_t[:, None, :]
    tables = [np.cos(angle_hw), np.sin(angle_hw), np.cos(angle_t), np.sin(angle_t)]
    return [jnp.asarray(table, jnp.float32) for table in tables] + [
        jnp.asarray(pairing, jnp.bfloat16)
    ]


def clip_span(counts_ref, clips, longest, frame):
    start = jnp.int32(0)
    stop = jnp.int32(1 << 30)
    end = jnp.int32(0)
    for clip in range(clips):
        end = end + counts_ref[clip]
        start = jnp.where(end <= frame, end, start)
        stop = jnp.where(end > frame, jnp.minimum(stop, end), stop)
    return jnp.clip(start, frame - (longest - 1), frame), stop


def kernel(
    dims,
    counts_ref,
    q_ref,
    k_ref,
    v_ref,
    w_ref,
    cos_hw_ref,
    sin_hw_ref,
    cos_t_ref,
    sin_t_ref,
    pairing_ref,
    out_ref,
    q_in,
    k_in,
    cos_hw,
    sin_hw,
    cos_t,
    sin_t,
    pairing,
    q_own,
    k_own,
    q_all,
    k_all,
    v_all,
    o_mine,
    o_all,
    w_all,
    total_ref,
    in_local,
    w_local,
    v_local,
    w_send,
    w_recv,
    k_send,
    k_recv,
    v_send,
    v_recv,
    q_send,
    q_recv,
    halo_send,
    halo_recv,
    o_send,
    o_recv,
    x_send,
    x_recv,
):
    heads, group, groups, peers, slots, longest, clips, own_frames = dims
    rows = own_frames * FRAME
    halo = longest - 1
    span = group * own_frames
    reach = (halo + span - 1) // span
    columns = out_ref.shape[1]
    position = lax.axis_index("seq")
    tp = lax.axis_index("tp")
    plane = position // group
    member = position % group
    first_frame = plane * span

    def head_of(who, slot):
        return lax.rem(who - 2 * tp + 2 * group * peers, group) + slot * group

    def sized(slot):
        return min(group, heads - slot * group)

    def to_member(d):
        return lax.rem(member + d, group)

    def from_member(d):
        return lax.rem(member - d + group, group)

    def device(seq, core):
        return (seq, core)

    loads = [
        pltpu.make_async_copy(source, target, in_local.at[i])
        for i, (source, target) in enumerate(
            [
                (cos_hw_ref, cos_hw),
                (sin_hw_ref, sin_hw),
                (cos_t_ref, cos_t),
                (sin_t_ref, sin_t),
                (pairing_ref, pairing),
                (k_ref, k_in),
                (q_ref, q_in),
            ]
        )
    ]
    for load in loads:
        load.start()

    barrier = pltpu.get_barrier_semaphore()
    for d in range(1, group):
        pl.semaphore_signal(
            barrier, inc=1, device_id=device(plane * group + to_member(d), tp), device_id_type=MESH
        )
    for d in range(1, peers):
        pl.semaphore_signal(
            barrier, inc=1, device_id=device(position, lax.rem(tp + d, peers)), device_id_type=MESH
        )
    greeted = jnp.int32(group - 1 + peers - 1)
    for d in range(1, reach + 1):
        above = plane + d < groups
        below = plane - d >= 0

        @pl.when(above)
        def _():
            pl.semaphore_signal(
                barrier, inc=1, device_id=device(position + d * group, tp), device_id_type=MESH
            )

        @pl.when(below)
        def _():
            pl.semaphore_signal(
                barrier, inc=1, device_id=device(position - d * group, tp), device_id_type=MESH
            )

        greeted = greeted + above.astype(jnp.int32) + below.astype(jnp.int32)
    pl.semaphore_wait(barrier, greeted)

    cosines, sines = [], []

    def rotated(ref, f, head):
        x = ref[f * FRAME : (f + 1) * FRAME, head * HEAD_DIM : (head + 1) * HEAD_DIM]
        paired = jnp.dot(x, pairing[...], preferred_element_type=jnp.float32)
        return (x.astype(jnp.float32) * cosines[f] + paired * sines[f]).astype(jnp.bfloat16)

    def own_rows(who):
        return pl.ds(halo + who * own_frames, own_frames)

    def query_rows(who):
        return pl.ds(pl.multiple_of(who * rows, rows), rows)

    def lanes_of(head):
        return pl.ds(pl.multiple_of(head * HEAD_DIM, HEAD_DIM), HEAD_DIM)

    def k_copy(slot, d, source, target):
        return pltpu.make_async_remote_copy(
            src_ref=k_own.at[head_of(target, slot)],
            dst_ref=k_all[slot].at[own_rows(source)],
            send_sem=k_send.at[slot, d],
            recv_sem=k_recv.at[slot, d],
            device_id=device(plane * group + target, tp),
            device_id_type=MESH,
        )

    def v_copy(slot, d, source, target):
        return pltpu.make_async_remote_copy(
            src_ref=v_ref.at[:, :, lanes_of(head_of(target, slot))],
            dst_ref=v_all[slot].at[own_rows(source)],
            send_sem=v_send.at[slot, d],
            recv_sem=v_recv.at[slot, d],
            device_id=device(plane * group + target, tp),
            device_id_type=MESH,
        )

    def v_stay(slot):
        return pltpu.make_async_copy(
            v_ref.at[:, :, lanes_of(head_of(member, slot))],
            v_all[slot].at[own_rows(member)],
            v_local.at[slot],
        )

    def q_copy(slot, d, source, target):
        return pltpu.make_async_remote_copy(
            src_ref=q_own.at[head_of(target, slot)],
            dst_ref=q_all.at[slot, query_rows(source), :],
            send_sem=q_send.at[slot, d],
            recv_sem=q_recv.at[slot, d],
            device_id=device(plane * group + target, tp),
            device_id_type=MESH,
        )

    def o_copy(slot, d, source, target):
        return pltpu.make_async_remote_copy(
            src_ref=o_mine.at[slot, query_rows(target), :],
            dst_ref=o_all.at[tp, head_of(source, slot)],
            send_sem=o_send.at[slot, d],
            recv_sem=o_recv.at[slot, d],
            device_id=device(plane * group + target, tp),
            device_id_type=MESH,
        )

    def w_copy(d):
        target = lax.rem(tp + d, peers)
        return pltpu.make_async_remote_copy(
            src_ref=w_ref.at[:, pl.ds(pl.multiple_of(target * columns, columns), columns)],
            dst_ref=w_all.at[tp],
            send_sem=w_send.at[d],
            recv_sem=w_recv.at[d],
            device_id=device(position, target),
            device_id_type=MESH,
        )

    def w_arrival(d):
        source = lax.rem(tp - d + peers, peers)
        return pltpu.make_async_remote_copy(
            src_ref=w_ref.at[:, pl.ds(pl.multiple_of(tp * columns, columns), columns)],
            dst_ref=w_all.at[source],
            send_sem=w_send.at[d],
            recv_sem=w_recv.at[d],
            device_id=device(position, source),
            device_id_type=MESH,
        )

    def x_copy(slot, d, source, target):
        span_heads = pl.ds(slot * group, sized(slot))
        return pltpu.make_async_remote_copy(
            src_ref=o_all.at[source, span_heads],
            dst_ref=o_all.at[source, span_heads],
            send_sem=x_send.at[slot, d],
            recv_sem=x_recv.at[slot, d],
            device_id=device(position, target),
            device_id_type=MESH,
        )

    def halo_frames(d):
        return min(span, halo - span * (d - 1))

    def halo_copy(slot, what, d, upward, arriving):
        n = halo_frames(d)
        if upward:
            src_frame, dst_frame = halo + span - n, span - n - span * d + halo
        else:
            src_frame, dst_frame = halo, halo + span * d
        which = 2 * (d - 1) + (0 if upward else 1)
        away = d * group if upward != arriving else -d * group
        buffer = (k_all, v_all)[what][slot]
        return pltpu.make_async_remote_copy(
            src_ref=buffer.at[pl.ds(src_frame, n)],
            dst_ref=buffer.at[pl.ds(dst_frame, n)],
            send_sem=halo_send.at[slot, what, which],
            recv_sem=halo_recv.at[slot, what, which],
            device_id=device(position + away, tp),
            device_id_type=MESH,
        )

    def exists(d, up):
        return plane + d < groups if up else plane - d >= 0

    have = [head_of(member, slot) < heads for slot in range(slots)]

    def angles():
        lane = lax.broadcasted_iota(jnp.int32, (FRAME, HEAD_DIM), 1)
        in_t = lane < SECTIONS[0]
        for f in range(own_frames):
            frame = position * own_frames + f
            t = frame - clip_span(counts_ref, clips, longest, frame)[0]
            cosines.append(jnp.where(in_t, cos_t[t], cos_hw[...]))
            sines.append(jnp.where(in_t, sin_t[t], sin_hw[...]))

    def send(copy, slot):
        for d in range(1, group):
            target = to_member(d)

            @pl.when(head_of(target, slot) < heads)
            def _():
                copy(slot, d, member, target).start()

    own_weight = pltpu.make_async_copy(
        w_ref.at[:, pl.ds(pl.multiple_of(tp * columns, columns), columns)],
        w_all.at[tp],
        w_local,
    )

    for slot in range(slots):
        slot_heads = range(slot * group, slot * group + sized(slot))
        send(v_copy, slot)

        @pl.when(have[slot])
        def _():
            v_stay(slot).start()

        if slot == 0:
            for load in loads[:-1]:
                load.wait()
            angles()
        for head in slot_heads:
            for f in range(own_frames):
                k_own[head, f] = rotated(k_in, f, head)
        send(k_copy, slot)

    loads[-1].wait()
    for slot in range(slots):
        for head in range(slot * group, slot * group + sized(slot)):
            for f in range(own_frames):
                part = slice(f * FRAME, (f + 1) * FRAME)
                q_own[head, part, :] = rotated(q_in, f, head)
        send(q_copy, slot)

    scale = HEAD_DIM**-0.5 * math.log2(math.e)

    def start_halos(slot, what):
        for d in range(1, reach + 1):
            for up in (True, False):

                @pl.when(exists(d, up))
                def _():
                    halo_copy(slot, what, d, up, False).start()

    def spread(slot):
        mine = head_of(member, slot)
        k_all[slot][own_rows(member)] = k_own[mine]
        q_all[slot, query_rows(member), :] = q_own[mine]
        for d in range(1, reach + 1):
            for up in (True, False):

                @pl.when(jnp.logical_not(exists(d, up)))
                def _():
                    n = halo_frames(d)
                    blank = halo + span * d if up else span - n - span * d + halo
                    for buffer in (k_all, v_all):
                        buffer[slot][blank : blank + n] = jnp.zeros(
                            (n, FRAME, HEAD_DIM), jnp.bfloat16
                        )

        v_stay(slot).wait()
        for d in range(1, group):
            v_copy(slot, d, from_member(d), member).wait_recv()
        start_halos(slot, 1)
        for d in range(1, group):
            k_copy(slot, d, from_member(d), member).wait_recv()
        start_halos(slot, 0)

    def settle(slot):
        for what in (1, 0):
            for d in range(1, reach + 1):
                for up in (True, False):

                    @pl.when(exists(d, not up))
                    def _():
                        halo_copy(slot, what, d, up, True).wait_recv()

    ones = jnp.ones((FRAME, HEAD_DIM), jnp.bfloat16)

    def attend(slot, d, carry):
        target = from_member(d)

        @pl.when(d > 0)
        def _():
            q_copy(slot, d, target, member).wait_recv()

        for f in range(own_frames):
            place = target * own_frames + f
            start, stop = clip_span(counts_ref, clips, longest, first_frame + place)
            here = pl.ds(pl.multiple_of(place * FRAME, FRAME), FRAME)
            first_key = start - first_frame + halo
            queries = q_all[slot, here, :]
            scores, tops, values, inside = [], [], [], []
            largest = None
            for i in range(longest):
                part = lax.dot_general(
                    queries,
                    k_all[slot][first_key + i],
                    (((1,), (1,)), ((), ())),
                    preferred_element_type=jnp.float32,
                )
                top = jnp.max(part, axis=1, keepdims=True)
                same = jnp.full((FRAME, 1), start + i, jnp.int32) < stop
                kept = jnp.where(same, top, NEG_FILL)
                largest = kept if i == 0 else jnp.maximum(largest, kept)
                both = jnp.concatenate([v_all[slot][first_key + i], ones], axis=1)
                in_clip = jnp.full(both.shape, start + i, jnp.int32) < stop
                scores.append(part)
                tops.append(top)
                inside.append(same)
                values.append(jnp.where(in_clip, both, jnp.zeros_like(both)))
            weights = [
                jnp.exp2((part - jnp.where(same, largest, top)) * scale).astype(jnp.bfloat16)
                for part, same, top in zip(scores, inside, tops)
            ]
            summed = jnp.dot(
                jnp.concatenate(weights, axis=1),
                jnp.concatenate(values, axis=0),
                preferred_element_type=jnp.float32,
            )
            o_mine[slot, here, :] = (
                summed[:, :HEAD_DIM] / summed[:, HEAD_DIM:]
            ).astype(jnp.bfloat16)

        @pl.when(d > 0)
        def _():
            o_copy(slot, group - d, member, target).start()

        return carry

    for slot in range(slots):

        @pl.when(have[slot])
        def _():
            spread(slot)

    for slot in range(slots):

        @pl.when(have[slot])
        def _():
            settle(slot)
            lax.fori_loop(0, 1, functools.partial(attend, slot), 0)
            o_all[tp, head_of(member, slot)] = o_mine[slot, query_rows(member), :]

        if slot == 0:
            own_weight.start()
            for d in range(1, peers):
                w_copy(d).start()

    for slot in range(slots):

        @pl.when(have[slot])
        def _():
            lax.fori_loop(1, group, functools.partial(attend, slot), 0)

    chunk = 256

    def project(source, slot, first, last):
        slot_heads = range(slot * group, slot * group + sized(slot))
        left = jnp.concatenate([o_all[source, head] for head in slot_heads], axis=1)
        deep = slice(slot * group * HEAD_DIM, (slot * group + sized(slot)) * HEAD_DIM)

        def body(step, carry):
            place = pl.ds(pl.multiple_of(step * chunk, chunk), chunk)
            term = jnp.dot(left, w_all[source, deep, place], preferred_element_type=jnp.float32)
            if not first:
                term = total_ref[:, place] + term
            if last:
                out_ref[:, place] = term.astype(jnp.bfloat16)
            else:
                total_ref[:, place] = term
            return carry

        lax.fori_loop(0, columns // chunk, body, 0)

    own_weight.wait()
    for slot in range(slots):
        for d in range(1, group):
            source = from_member(d)

            @pl.when(head_of(source, slot) < heads)
            def _():
                o_copy(slot, d, source, member).wait_recv()

        for d in range(1, peers):
            x_copy(slot, d, tp, lax.rem(tp + d, peers)).start()
        project(tp, slot, slot == 0, peers == 1 and slot == slots - 1)

    for d in range(1, peers):
        w_arrival(d).wait_recv()
    for slot in range(slots):
        for d in range(1, peers):
            source = lax.rem(tp - d + peers, peers)
            x_copy(slot, d, source, tp).wait_recv()
            project(source, slot, False, slot == slots - 1 and d == peers - 1)

    for d in range(1, peers):
        w_copy(d).wait_send()
    for slot in range(slots):
        for d in range(1, peers):
            x_copy(slot, d, tp, lax.rem(tp + d, peers)).wait_send()
        for d in range(1, group):
            target = to_member(d)

            @pl.when(head_of(target, slot) < heads)
            def _():
                k_copy(slot, d, member, target).wait_send()
                v_copy(slot, d, member, target).wait_send()
                q_copy(slot, d, member, target).wait_send()

            @pl.when(have[slot])
            def _():
                o_copy(slot, d, member, target).wait_send()

        for d in range(1, reach + 1):
            for up in (True, False):

                @pl.when(have[slot] & exists(d, up))
                def _():
                    for what in (0, 1):
                        halo_copy(slot, what, d, up, False).wait_send()


def per_device(seq, peers, query_rows, key_rows, value_rows, frame_counts, out_weight):
    rows, features = query_rows.shape
    heads = features // HEAD_DIM
    own_frames = rows // FRAME
    longest = own_frames * seq // 8
    group = 4
    groups = seq // group
    slots = -(-heads // group)
    columns = out_weight.shape[1] // peers
    clips = frame_counts.shape[0]
    span = group * own_frames
    halo = longest - 1
    reach = -(-halo // span)
    dims = (heads, group, groups, peers, slots, longest, clips, own_frames)
    value_frames = value_rows.reshape(own_frames, FRAME, features)
    vmem = pl.BlockSpec(memory_space=pltpu.VMEM)
    dma = pltpu.SemaphoreType.DMA
    bf16 = jnp.bfloat16
    flops = 2 * rows * features * out_weight.shape[1]
    return pl.pallas_call(
        functools.partial(kernel, dims),
        out_shape=jax.ShapeDtypeStruct((rows, columns), bf16),
        in_specs=[
            pl.BlockSpec(memory_space=pltpu.SMEM),
        ]
        + [pl.BlockSpec(memory_space=pl.ANY)] * 9,
        out_specs=vmem,
        scratch_shapes=[
            pltpu.VMEM((rows, features), bf16),
            pltpu.VMEM((rows, features), bf16),
            pltpu.VMEM((FRAME, HEAD_DIM), jnp.float32),
            pltpu.VMEM((FRAME, HEAD_DIM), jnp.float32),
            pltpu.VMEM((longest, 1, HEAD_DIM), jnp.float32),
            pltpu.VMEM((longest, 1, HEAD_DIM), jnp.float32),
            pltpu.VMEM((HEAD_DIM, HEAD_DIM), bf16),
            pltpu.VMEM((heads, rows, HEAD_DIM), bf16),
            pltpu.VMEM((heads, own_frames, FRAME, HEAD_DIM), bf16),
            pltpu.VMEM((slots, group * rows, HEAD_DIM), bf16),
            [pltpu.VMEM((span + 2 * halo, FRAME, HEAD_DIM), bf16)] * slots,
            [pltpu.VMEM((span + 2 * halo, FRAME, HEAD_DIM), bf16)] * slots,
            pltpu.VMEM((slots, group * rows, HEAD_DIM), bf16),
            pltpu.VMEM((peers, heads, rows, HEAD_DIM), bf16),
            pltpu.VMEM((peers, features, columns), bf16),
            pltpu.VMEM((rows, columns), jnp.float32),
            dma((7,)),
            dma(()),
            dma((slots,)),
            dma((peers,)),
            dma((peers,)),
            dma((slots, group)),
            dma((slots, group)),
            dma((slots, group)),
            dma((slots, group)),
            dma((slots, group)),
            dma((slots, group)),
            dma((slots, 2, 2 * reach)),
            dma((slots, 2, 2 * reach)),
            dma((slots, group)),
            dma((slots, group)),
            dma((slots, peers)),
            dma((slots, peers)),
        ],
        compiler_params=pltpu.CompilerParams(
            collective_id=0, has_side_effects=True, vmem_limit_bytes=56 * 1024 * 1024
        ),
        cost_estimate=pl.CostEstimate(flops=flops, bytes_accessed=8 << 20, transcendentals=0),
    )(frame_counts, query_rows, key_rows, value_frames, out_weight, *rope_tables(longest))


def solution(mesh):
    return jax.shard_map(
        functools.partial(per_device, mesh.shape["seq"], mesh.shape["tp"]),
        mesh=mesh,
        in_specs=(P("seq", "tp"), P("seq", "tp"), P("seq", "tp"), P(), P("tp", None)),
        out_specs=P("seq", "tp"),
        check_vma=False,
    )
```

```python
import functools
import math

import jax
import jax.numpy as jnp
import numpy as np
from jax import lax
from jax.experimental import pallas as pl
from jax.experimental.pallas import tpu as pltpu
from jax.sharding import PartitionSpec as P

SECTIONS = (16, 56, 56)
PH = 16
PW = 16
FRAME = PH * PW
HEAD_DIM = 128
ROPE_BASE = 256.0
NEG_FILL = -1e30
MESH = pl.DeviceIdType.MESH


def rope_tables(longest):
    angle_hw = np.zeros((FRAME, HEAD_DIM), np.float64)
    angle_t = np.zeros((longest, HEAD_DIM), np.float64)
    pairing = np.zeros((HEAD_DIM, HEAD_DIM), np.float32)
    row = np.arange(FRAME)
    first = 0
    for section, width in enumerate(SECTIONS):
        half = width // 2
        frequency = np.exp(-(2.0 * np.arange(half) / width) * math.log(ROPE_BASE))
        frequency = np.concatenate([frequency, frequency])
        lanes = slice(first, first + width)
        if section == 0:
            angle_t[:, lanes] = np.arange(longest)[:, None] * frequency[None, :]
        else:
            place = row // PW if section == 1 else row % PW
            angle_hw[:, lanes] = place[:, None] * frequency[None, :]
        for j in range(half):
            pairing[first + half + j, first + j] = -1.0
            pairing[first + j, first + half + j] = 1.0
        first += width
    angle_t = angle_t[:, None, :]
    tables = [np.cos(angle_hw), np.sin(angle_hw), np.cos(angle_t), np.sin(angle_t)]
    return [jnp.asarray(table, jnp.float32) for table in tables] + [
        jnp.asarray(pairing, jnp.bfloat16)
    ]


def clip_span(counts_ref, clips, longest, frame):
    start = jnp.int32(0)
    stop = jnp.int32(1 << 30)
    end = jnp.int32(0)
    for clip in range(clips):
        end = end + counts_ref[clip]
        start = jnp.where(end <= frame, end, start)
        stop = jnp.where(end > frame, jnp.minimum(stop, end), stop)
    return jnp.clip(start, frame - (longest - 1), frame), stop


def kernel(
    dims,
    counts_ref,
    q_ref,
    k_ref,
    v_ref,
    w_ref,
    cos_hw_ref,
    sin_hw_ref,
    cos_t_ref,
    sin_t_ref,
    pairing_ref,
    out_ref,
    q_in,
    k_in,
    cos_hw,
    sin_hw,
    cos_t,
    sin_t,
    pairing,
    q_own,
    k_own,
    q_all,
    k_all,
    v_all,
    v_turned,
    o_mine,
    o_all,
    w_all,
    total_ref,
    in_local,
    w_local,
    v_local,
    w_send,
    w_recv,
    k_send,
    k_recv,
    v_send,
    v_recv,
    q_send,
    q_recv,
    halo_send,
    halo_recv,
    o_send,
    o_recv,
    x_send,
    x_recv,
):
    heads, group, groups, peers, slots, longest, clips, own_frames = dims
    rows = own_frames * FRAME
    halo = longest - 1
    span = group * own_frames
    reach = (halo + span - 1) // span
    columns = out_ref.shape[1]
    position = lax.axis_index("seq")
    tp = lax.axis_index("tp")
    plane = position // group
    member = position % group
    first_frame = plane * span

    def head_of(who, slot):
        return lax.rem(who - 2 * tp + 2 * group * peers, group) + slot * group

    def sized(slot):
        return min(group, heads - slot * group)

    def to_member(d):
        return lax.rem(member + d, group)

    def from_member(d):
        return lax.rem(member - d + group, group)

    def device(seq, core):
        return (seq, core)

    loads = [
        pltpu.make_async_copy(source, target, in_local.at[i])
        for i, (source, target) in enumerate(
            [
                (cos_hw_ref, cos_hw),
                (sin_hw_ref, sin_hw),
                (cos_t_ref, cos_t),
                (sin_t_ref, sin_t),
                (pairing_ref, pairing),
                (k_ref, k_in),
                (q_ref, q_in),
            ]
        )
    ]
    for load in loads:
        load.start()

    barrier = pltpu.get_barrier_semaphore()
    for d in range(1, group):
        pl.semaphore_signal(
            barrier, inc=1, device_id=device(plane * group + to_member(d), tp), device_id_type=MESH
        )
    for d in range(1, peers):
        pl.semaphore_signal(
            barrier, inc=1, device_id=device(position, lax.rem(tp + d, peers)), device_id_type=MESH
        )
    greeted = jnp.int32(group - 1 + peers - 1)
    for d in range(1, reach + 1):
        above = plane + d < groups
        below = plane - d >= 0

        @pl.when(above)
        def _():
            pl.semaphore_signal(
                barrier, inc=1, device_id=device(position + d * group, tp), device_id_type=MESH
            )

        @pl.when(below)
        def _():
            pl.semaphore_signal(
                barrier, inc=1, device_id=device(position - d * group, tp), device_id_type=MESH
            )

        greeted = greeted + above.astype(jnp.int32) + below.astype(jnp.int32)
    pl.semaphore_wait(barrier, greeted)

    cosines, sines = [], []

    def rotated(ref, f, head):
        x = ref[f * FRAME : (f + 1) * FRAME, head * HEAD_DIM : (head + 1) * HEAD_DIM]
        paired = jnp.dot(x, pairing[...], preferred_element_type=jnp.float32)
        return (x.astype(jnp.float32) * cosines[f] + paired * sines[f]).astype(jnp.bfloat16)

    def own_rows(who):
        return pl.ds(halo + who * own_frames, own_frames)

    def query_rows(who):
        return pl.ds(pl.multiple_of(who * rows, rows), rows)

    def lanes_of(head):
        return pl.ds(pl.multiple_of(head * HEAD_DIM, HEAD_DIM), HEAD_DIM)

    def k_copy(slot, d, source, target):
        return pltpu.make_async_remote_copy(
            src_ref=k_own.at[head_of(target, slot)],
            dst_ref=k_all[slot].at[own_rows(source)],
            send_sem=k_send.at[slot, d],
            recv_sem=k_recv.at[slot, d],
            device_id=device(plane * group + target, tp),
            device_id_type=MESH,
        )

    def v_copy(slot, d, source, target):
        return pltpu.make_async_remote_copy(
            src_ref=v_ref.at[:, :, lanes_of(head_of(target, slot))],
            dst_ref=v_all[slot].at[own_rows(source)],
            send_sem=v_send.at[slot, d],
            recv_sem=v_recv.at[slot, d],
            device_id=device(plane * group + target, tp),
            device_id_type=MESH,
        )

    def v_stay(slot):
        return pltpu.make_async_copy(
            v_ref.at[:, :, lanes_of(head_of(member, slot))],
            v_all[slot].at[own_rows(member)],
            v_local.at[slot],
        )

    def q_copy(slot, d, source, target):
        return pltpu.make_async_remote_copy(
            src_ref=q_own.at[head_of(target, slot)],
            dst_ref=q_all.at[slot, query_rows(source), :],
            send_sem=q_send.at[slot, d],
            recv_sem=q_recv.at[slot, d],
            device_id=device(plane * group + target, tp),
            device_id_type=MESH,
        )

    def o_copy(slot, d, source, target):
        return pltpu.make_async_remote_copy(
            src_ref=o_mine.at[slot, query_rows(target), :],
            dst_ref=o_all.at[tp, head_of(source, slot)],
            send_sem=o_send.at[slot, d],
            recv_sem=o_recv.at[slot, d],
            device_id=device(plane * group + target, tp),
            device_id_type=MESH,
        )

    def w_copy(d):
        target = lax.rem(tp + d, peers)
        return pltpu.make_async_remote_copy(
            src_ref=w_ref.at[:, pl.ds(pl.multiple_of(target * columns, columns), columns)],
            dst_ref=w_all.at[tp],
            send_sem=w_send.at[d],
            recv_sem=w_recv.at[d],
            device_id=device(position, target),
            device_id_type=MESH,
        )

    def w_arrival(d):
        source = lax.rem(tp - d + peers, peers)
        return pltpu.make_async_remote_copy(
            src_ref=w_ref.at[:, pl.ds(pl.multiple_of(tp * columns, columns), columns)],
            dst_ref=w_all.at[source],
            send_sem=w_send.at[d],
            recv_sem=w_recv.at[d],
            device_id=device(position, source),
            device_id_type=MESH,
        )

    def x_copy(slot, d, source, target):
        span_heads = pl.ds(slot * group, sized(slot))
        return pltpu.make_async_remote_copy(
            src_ref=o_all.at[source, span_heads],
            dst_ref=o_all.at[source, span_heads],
            send_sem=x_send.at[slot, d],
            recv_sem=x_recv.at[slot, d],
            device_id=device(position, target),
            device_id_type=MESH,
        )

    def halo_frames(d):
        return min(span, halo - span * (d - 1))

    def halo_copy(slot, what, d, upward, arriving):
        n = halo_frames(d)
        if upward:
            src_frame, dst_frame = halo + span - n, span - n - span * d + halo
        else:
            src_frame, dst_frame = halo, halo + span * d
        which = 2 * (d - 1) + (0 if upward else 1)
        away = d * group if upward != arriving else -d * group
        buffer = (k_all, v_all)[what][slot]
        return pltpu.make_async_remote_copy(
            src_ref=buffer.at[pl.ds(src_frame, n)],
            dst_ref=buffer.at[pl.ds(dst_frame, n)],
            send_sem=halo_send.at[slot, what, which],
            recv_sem=halo_recv.at[slot, what, which],
            device_id=device(position + away, tp),
            device_id_type=MESH,
        )

    def exists(d, up):
        return plane + d < groups if up else plane - d >= 0

    have = [head_of(member, slot) < heads for slot in range(slots)]

    def angles():
        lane = lax.broadcasted_iota(jnp.int32, (FRAME, HEAD_DIM), 1)
        in_t = lane < SECTIONS[0]
        for f in range(own_frames):
            frame = position * own_frames + f
            t = frame - clip_span(counts_ref, clips, longest, frame)[0]
            cosines.append(jnp.where(in_t, cos_t[t], cos_hw[...]))
            sines.append(jnp.where(in_t, sin_t[t], sin_hw[...]))

    def send(copy, slot):
        for d in range(1, group):
            target = to_member(d)

            @pl.when(head_of(target, slot) < heads)
            def _():
                copy(slot, d, member, target).start()

    own_weight = pltpu.make_async_copy(
        w_ref.at[:, pl.ds(pl.multiple_of(tp * columns, columns), columns)],
        w_all.at[tp],
        w_local,
    )

    for slot in range(slots):
        slot_heads = range(slot * group, slot * group + sized(slot))
        send(v_copy, slot)

        @pl.when(have[slot])
        def _():
            v_stay(slot).start()

        if slot == 0:
            for load in loads[:-1]:
                load.wait()
            angles()
        for head in slot_heads:
            for f in range(own_frames):
                k_own[head, f] = rotated(k_in, f, head)
        send(k_copy, slot)

    loads[-1].wait()
    for slot in range(slots):
        for head in range(slot * group, slot * group + sized(slot)):
            for f in range(own_frames):
                part = slice(f * FRAME, (f + 1) * FRAME)
                q_own[head, part, :] = rotated(q_in, f, head)
        send(q_copy, slot)

    scale = HEAD_DIM**-0.5 * math.log2(math.e)

    def start_halos(slot, what):
        for d in range(1, reach + 1):
            for up in (True, False):

                @pl.when(exists(d, up))
                def _():
                    halo_copy(slot, what, d, up, False).start()

    def spread(slot):
        mine = head_of(member, slot)
        k_all[slot][own_rows(member)] = k_own[mine]
        q_all[slot, query_rows(member), :] = q_own[mine]
        for d in range(1, reach + 1):
            for up in (True, False):

                @pl.when(jnp.logical_not(exists(d, up)))
                def _():
                    n = halo_frames(d)
                    blank = halo + span * d if up else span - n - span * d + halo
                    for buffer in (k_all, v_all):
                        buffer[slot][blank : blank + n] = jnp.zeros(
                            (n, FRAME, HEAD_DIM), jnp.bfloat16
                        )

        v_stay(slot).wait()
        for d in range(1, group):
            v_copy(slot, d, from_member(d), member).wait_recv()
        start_halos(slot, 1)
        for d in range(1, group):
            k_copy(slot, d, from_member(d), member).wait_recv()
        start_halos(slot, 0)

    def settle(slot):
        for what in (1, 0):
            for d in range(1, reach + 1):
                for up in (True, False):

                    @pl.when(exists(d, not up))
                    def _():
                        halo_copy(slot, what, d, up, True).wait_recv()

    def turn(slot):
        def body(frame, carry):
            v_turned[slot][frame, :HEAD_DIM, :] = v_all[slot][frame].T
            v_turned[slot][frame, HEAD_DIM:, :] = jnp.ones((16, FRAME), jnp.bfloat16)
            return carry

        lax.fori_loop(0, span + 2 * halo, body, 0)

    def attend(slot, d, carry):
        target = from_member(d)

        @pl.when(d > 0)
        def _():
            q_copy(slot, d, target, member).wait_recv()

        for f in range(own_frames):
            place = target * own_frames + f
            start, stop = clip_span(counts_ref, clips, longest, first_frame + place)
            here = pl.ds(pl.multiple_of(place * FRAME, FRAME), FRAME)
            first_key = start - first_frame + halo
            queries = q_all[slot, here, :]
            scores, tops, values, inside = [], [], [], []
            largest = None
            for i in range(longest):
                part = lax.dot_general(
                    k_all[slot][first_key + i],
                    queries,
                    (((1,), (1,)), ((), ())),
                    preferred_element_type=jnp.float32,
                )
                top = jnp.max(part, axis=0, keepdims=True)
                same = jnp.full((1, FRAME), start + i, jnp.int32) < stop
                kept = jnp.where(same, top, NEG_FILL)
                largest = kept if i == 0 else jnp.maximum(largest, kept)
                turned = v_turned[slot][first_key + i]
                in_clip = jnp.full(turned.shape, start + i, jnp.int32) < stop
                scores.append(part)
                tops.append(top)
                inside.append(same)
                values.append(jnp.where(in_clip, turned, jnp.zeros_like(turned)))
            weights = [
                jnp.exp2((part - jnp.where(same, largest, top)) * scale).astype(jnp.bfloat16)
                for part, same, top in zip(scores, inside, tops)
            ]
            summed = jnp.dot(
                jnp.concatenate(values, axis=1),
                jnp.concatenate(weights, axis=0),
                preferred_element_type=jnp.float32,
            )
            attended = summed[:HEAD_DIM] / summed[HEAD_DIM : HEAD_DIM + 1]
            o_mine[slot, here, :] = attended.T.astype(jnp.bfloat16)

        @pl.when(d > 0)
        def _():
            o_copy(slot, group - d, member, target).start()

        return carry

    for slot in range(slots):

        @pl.when(have[slot])
        def _():
            spread(slot)

    for slot in range(slots):

        @pl.when(have[slot])
        def _():
            settle(slot)
            turn(slot)
            lax.fori_loop(0, 1, functools.partial(attend, slot), 0)
            o_all[tp, head_of(member, slot)] = o_mine[slot, query_rows(member), :]

        if slot == 0:
            own_weight.start()
            for d in range(1, peers):
                w_copy(d).start()

    for slot in range(slots):

        @pl.when(have[slot])
        def _():
            lax.fori_loop(1, group, functools.partial(attend, slot), 0)

    chunk = 256

    def project(source, slot, first, last):
        slot_heads = range(slot * group, slot * group + sized(slot))
        left = jnp.concatenate([o_all[source, head] for head in slot_heads], axis=1)
        deep = slice(slot * group * HEAD_DIM, (slot * group + sized(slot)) * HEAD_DIM)

        def body(step, carry):
            place = pl.ds(pl.multiple_of(step * chunk, chunk), chunk)
            term = jnp.dot(left, w_all[source, deep, place], preferred_element_type=jnp.float32)
            if not first:
                term = total_ref[:, place] + term
            if last:
                out_ref[:, place] = term.astype(jnp.bfloat16)
            else:
                total_ref[:, place] = term
            return carry

        lax.fori_loop(0, columns // chunk, body, 0)

    own_weight.wait()
    for slot in range(slots):
        for d in range(1, group):
            source = from_member(d)

            @pl.when(head_of(source, slot) < heads)
            def _():
                o_copy(slot, d, source, member).wait_recv()

        for d in range(1, peers):
            x_copy(slot, d, tp, lax.rem(tp + d, peers)).start()
        project(tp, slot, slot == 0, peers == 1 and slot == slots - 1)

    for d in range(1, peers):
        w_arrival(d).wait_recv()
    for slot in range(slots):
        for d in range(1, peers):
            source = lax.rem(tp - d + peers, peers)
            x_copy(slot, d, source, tp).wait_recv()
            project(source, slot, False, slot == slots - 1 and d == peers - 1)

    for d in range(1, peers):
        w_copy(d).wait_send()
    for slot in range(slots):
        for d in range(1, peers):
            x_copy(slot, d, tp, lax.rem(tp + d, peers)).wait_send()
        for d in range(1, group):
            target = to_member(d)

            @pl.when(head_of(target, slot) < heads)
            def _():
                k_copy(slot, d, member, target).wait_send()
                v_copy(slot, d, member, target).wait_send()
                q_copy(slot, d, member, target).wait_send()

            @pl.when(have[slot])
            def _():
                o_copy(slot, d, member, target).wait_send()

        for d in range(1, reach + 1):
            for up in (True, False):

                @pl.when(have[slot] & exists(d, up))
                def _():
                    for what in (0, 1):
                        halo_copy(slot, what, d, up, False).wait_send()


def per_device(seq, peers, query_rows, key_rows, value_rows, frame_counts, out_weight):
    rows, features = query_rows.shape
    heads = features // HEAD_DIM
    own_frames = rows // FRAME
    longest = own_frames * seq // 8
    group = 4
    groups = seq // group
    slots = -(-heads // group)
    columns = out_weight.shape[1] // peers
    clips = frame_counts.shape[0]
    span = group * own_frames
    halo = longest - 1
    reach = -(-halo // span)
    dims = (heads, group, groups, peers, slots, longest, clips, own_frames)
    value_frames = value_rows.reshape(own_frames, FRAME, features)
    vmem = pl.BlockSpec(memory_space=pltpu.VMEM)
    dma = pltpu.SemaphoreType.DMA
    bf16 = jnp.bfloat16
    flops = 2 * rows * features * out_weight.shape[1]
    return pl.pallas_call(
        functools.partial(kernel, dims),
        out_shape=jax.ShapeDtypeStruct((rows, columns), bf16),
        in_specs=[
            pl.BlockSpec(memory_space=pltpu.SMEM),
        ]
        + [pl.BlockSpec(memory_space=pl.ANY)] * 9,
        out_specs=vmem,
        scratch_shapes=[
            pltpu.VMEM((rows, features), bf16),
            pltpu.VMEM((rows, features), bf16),
            pltpu.VMEM((FRAME, HEAD_DIM), jnp.float32),
            pltpu.VMEM((FRAME, HEAD_DIM), jnp.float32),
            pltpu.VMEM((longest, 1, HEAD_DIM), jnp.float32),
            pltpu.VMEM((longest, 1, HEAD_DIM), jnp.float32),
            pltpu.VMEM((HEAD_DIM, HEAD_DIM), bf16),
            pltpu.VMEM((heads, rows, HEAD_DIM), bf16),
            pltpu.VMEM((heads, own_frames, FRAME, HEAD_DIM), bf16),
            pltpu.VMEM((slots, group * rows, HEAD_DIM), bf16),
            [pltpu.VMEM((span + 2 * halo, FRAME, HEAD_DIM), bf16)] * slots,
            [pltpu.VMEM((span + 2 * halo, FRAME, HEAD_DIM), bf16)] * slots,
            [pltpu.VMEM((span + 2 * halo, HEAD_DIM + 16, FRAME), bf16)] * slots,
            pltpu.VMEM((slots, group * rows, HEAD_DIM), bf16),
            pltpu.VMEM((peers, heads, rows, HEAD_DIM), bf16),
            pltpu.VMEM((peers, features, columns), bf16),
            pltpu.VMEM((rows, columns), jnp.float32),
            dma((7,)),
            dma(()),
            dma((slots,)),
            dma((peers,)),
            dma((peers,)),
            dma((slots, group)),
            dma((slots, group)),
            dma((slots, group)),
            dma((slots, group)),
            dma((slots, group)),
            dma((slots, group)),
            dma((slots, 2, 2 * reach)),
            dma((slots, 2, 2 * reach)),
            dma((slots, group)),
            dma((slots, group)),
            dma((slots, peers)),
            dma((slots, peers)),
        ],
        compiler_params=pltpu.CompilerParams(
            collective_id=0, has_side_effects=True, vmem_limit_bytes=56 * 1024 * 1024
        ),
        cost_estimate=pl.CostEstimate(flops=flops, bytes_accessed=8 << 20, transcendentals=0),
    )(frame_counts, query_rows, key_rows, value_frames, out_weight, *rope_tables(longest))


def solution(mesh):
    return jax.shard_map(
        functools.partial(per_device, mesh.shape["seq"], mesh.shape["tp"]),
        mesh=mesh,
        in_specs=(P("seq", "tp"), P("seq", "tp"), P("seq", "tp"), P(), P("tp", None)),
        out_specs=P("seq", "tp"),
        check_vma=False,
    )
```

```python
import functools
import math

import jax
import jax.numpy as jnp
import numpy as np
from jax import lax
from jax.experimental import pallas as pl
from jax.experimental.pallas import tpu as pltpu
from jax.sharding import PartitionSpec as P

SECTIONS = (16, 56, 56)
PH = 16
PW = 16
FRAME = PH * PW
HEAD_DIM = 128
ROPE_BASE = 256.0
NEG_FILL = -1e30
MESH = pl.DeviceIdType.MESH


def rope_tables(longest):
    angle_hw = np.zeros((FRAME, HEAD_DIM), np.float64)
    angle_t = np.zeros((longest, HEAD_DIM), np.float64)
    pairing = np.zeros((HEAD_DIM, HEAD_DIM), np.float32)
    row = np.arange(FRAME)
    first = 0
    for section, width in enumerate(SECTIONS):
        half = width // 2
        frequency = np.exp(-(2.0 * np.arange(half) / width) * math.log(ROPE_BASE))
        frequency = np.concatenate([frequency, frequency])
        lanes = slice(first, first + width)
        if section == 0:
            angle_t[:, lanes] = np.arange(longest)[:, None] * frequency[None, :]
        else:
            place = row // PW if section == 1 else row % PW
            angle_hw[:, lanes] = place[:, None] * frequency[None, :]
        for j in range(half):
            pairing[first + half + j, first + j] = -1.0
            pairing[first + j, first + half + j] = 1.0
        first += width
    angle_t = angle_t[:, None, :]
    tables = [np.cos(angle_hw), np.sin(angle_hw), np.cos(angle_t), np.sin(angle_t)]
    return [jnp.asarray(table, jnp.float32) for table in tables] + [
        jnp.asarray(pairing, jnp.bfloat16)
    ]


def clip_span(counts_ref, clips, longest, frame):
    start = jnp.int32(0)
    stop = jnp.int32(1 << 30)
    end = jnp.int32(0)
    for clip in range(clips):
        end = end + counts_ref[clip]
        start = jnp.where(end <= frame, end, start)
        stop = jnp.where(end > frame, jnp.minimum(stop, end), stop)
    return jnp.clip(start, frame - (longest - 1), frame), stop


def kernel(
    dims,
    counts_ref,
    q_ref,
    k_ref,
    v_ref,
    w_ref,
    cos_hw_ref,
    sin_hw_ref,
    cos_t_ref,
    sin_t_ref,
    pairing_ref,
    out_ref,
    q_in,
    k_in,
    cos_hw,
    sin_hw,
    cos_t,
    sin_t,
    pairing,
    q_own,
    k_own,
    q_all,
    k_all,
    v_all,
    o_mine,
    o_all,
    w_all,
    total_ref,
    in_local,
    w_local,
    v_local,
    w_send,
    w_recv,
    k_send,
    k_recv,
    v_send,
    v_recv,
    q_send,
    q_recv,
    halo_send,
    halo_recv,
    o_send,
    o_recv,
    x_send,
    x_recv,
):
    heads, group, groups, peers, slots, longest, clips, own_frames = dims
    rows = own_frames * FRAME
    halo = longest - 1
    span = group * own_frames
    reach = (halo + span - 1) // span
    columns = out_ref.shape[1]
    position = lax.axis_index("seq")
    tp = lax.axis_index("tp")
    plane = position // group
    member = position % group
    first_frame = plane * span

    def head_of(who, slot):
        return lax.rem(who - 2 * tp + 2 * group * peers, group) + slot * group

    def sized(slot):
        return min(group, heads - slot * group)

    def to_member(d):
        return lax.rem(member + d, group)

    def from_member(d):
        return lax.rem(member - d + group, group)

    def device(seq, core):
        return (seq, core)

    loads = [
        pltpu.make_async_copy(source, target, in_local.at[i])
        for i, (source, target) in enumerate(
            [
                (cos_hw_ref, cos_hw),
                (sin_hw_ref, sin_hw),
                (cos_t_ref, cos_t),
                (sin_t_ref, sin_t),
                (pairing_ref, pairing),
                (k_ref, k_in),
                (q_ref, q_in),
            ]
        )
    ]
    for load in loads:
        load.start()

    barrier = pltpu.get_barrier_semaphore()
    for d in range(1, group):
        pl.semaphore_signal(
            barrier, inc=1, device_id=device(plane * group + to_member(d), tp), device_id_type=MESH
        )
    for d in range(1, peers):
        pl.semaphore_signal(
            barrier, inc=1, device_id=device(position, lax.rem(tp + d, peers)), device_id_type=MESH
        )
    greeted = jnp.int32(group - 1 + peers - 1)
    for d in range(1, reach + 1):
        above = plane + d < groups
        below = plane - d >= 0

        @pl.when(above)
        def _():
            pl.semaphore_signal(
                barrier, inc=1, device_id=device(position + d * group, tp), device_id_type=MESH
            )

        @pl.when(below)
        def _():
            pl.semaphore_signal(
                barrier, inc=1, device_id=device(position - d * group, tp), device_id_type=MESH
            )

        greeted = greeted + above.astype(jnp.int32) + below.astype(jnp.int32)
    pl.semaphore_wait(barrier, greeted)

    cosines, sines = [], []

    def rotated(ref, f, head):
        x = ref[f * FRAME : (f + 1) * FRAME, head * HEAD_DIM : (head + 1) * HEAD_DIM]
        paired = jnp.dot(x, pairing[...], preferred_element_type=jnp.float32)
        return (x.astype(jnp.float32) * cosines[f] + paired * sines[f]).astype(jnp.bfloat16)

    def own_rows(who):
        return pl.ds(halo + who * own_frames, own_frames)

    def query_rows(who):
        return pl.ds(pl.multiple_of(who * rows, rows), rows)

    def lanes_of(head):
        return pl.ds(pl.multiple_of(head * HEAD_DIM, HEAD_DIM), HEAD_DIM)

    def k_copy(slot, d, source, target):
        return pltpu.make_async_remote_copy(
            src_ref=k_own.at[head_of(target, slot)],
            dst_ref=k_all[slot].at[own_rows(source)],
            send_sem=k_send.at[slot, d],
            recv_sem=k_recv.at[slot, d],
            device_id=device(plane * group + target, tp),
            device_id_type=MESH,
        )

    def v_copy(slot, d, source, target):
        return pltpu.make_async_remote_copy(
            src_ref=v_ref.at[:, :, lanes_of(head_of(target, slot))],
            dst_ref=v_all[slot].at[own_rows(source)],
            send_sem=v_send.at[slot, d],
            recv_sem=v_recv.at[slot, d],
            device_id=device(plane * group + target, tp),
            device_id_type=MESH,
        )

    def v_stay(slot):
        return pltpu.make_async_copy(
            v_ref.at[:, :, lanes_of(head_of(member, slot))],
            v_all[slot].at[own_rows(member)],
            v_local.at[slot],
        )

    def q_copy(slot, d, source, target):
        return pltpu.make_async_remote_copy(
            src_ref=q_own.at[head_of(target, slot)],
            dst_ref=q_all.at[slot, query_rows(source), :],
            send_sem=q_send.at[slot, d],
            recv_sem=q_recv.at[slot, d],
            device_id=device(plane * group + target, tp),
            device_id_type=MESH,
        )

    def o_copy(slot, d, source, target):
        return pltpu.make_async_remote_copy(
            src_ref=o_mine.at[slot, query_rows(target), :],
            dst_ref=o_all.at[tp, head_of(source, slot)],
            send_sem=o_send.at[slot, d],
            recv_sem=o_recv.at[slot, d],
            device_id=device(plane * group + target, tp),
            device_id_type=MESH,
        )

    def w_copy(d):
        target = lax.rem(tp + d, peers)
        return pltpu.make_async_remote_copy(
            src_ref=w_ref.at[:, pl.ds(pl.multiple_of(target * columns, columns), columns)],
            dst_ref=w_all.at[tp],
            send_sem=w_send.at[d],
            recv_sem=w_recv.at[d],
            device_id=device(position, target),
            device_id_type=MESH,
        )

    def w_arrival(d):
        source = lax.rem(tp - d + peers, peers)
        return pltpu.make_async_remote_copy(
            src_ref=w_ref.at[:, pl.ds(pl.multiple_of(tp * columns, columns), columns)],
            dst_ref=w_all.at[source],
            send_sem=w_send.at[d],
            recv_sem=w_recv.at[d],
            device_id=device(position, source),
            device_id_type=MESH,
        )

    def x_copy(slot, d, source, target):
        span_heads = pl.ds(slot * group, sized(slot))
        return pltpu.make_async_remote_copy(
            src_ref=o_all.at[source, span_heads],
            dst_ref=o_all.at[source, span_heads],
            send_sem=x_send.at[slot, d],
            recv_sem=x_recv.at[slot, d],
            device_id=device(position, target),
            device_id_type=MESH,
        )

    def halo_frames(d):
        return min(span, halo - span * (d - 1))

    def halo_copy(slot, what, d, upward, arriving):
        n = halo_frames(d)
        if upward:
            src_frame, dst_frame = halo + span - n, span - n - span * d + halo
        else:
            src_frame, dst_frame = halo, halo + span * d
        which = 2 * (d - 1) + (0 if upward else 1)
        away = d * group if upward != arriving else -d * group
        buffer = (k_all, v_all)[what][slot]
        return pltpu.make_async_remote_copy(
            src_ref=buffer.at[pl.ds(src_frame, n)],
            dst_ref=buffer.at[pl.ds(dst_frame, n)],
            send_sem=halo_send.at[slot, what, which],
            recv_sem=halo_recv.at[slot, what, which],
            device_id=device(position + away, tp),
            device_id_type=MESH,
        )

    def exists(d, up):
        return plane + d < groups if up else plane - d >= 0

    have = [head_of(member, slot) < heads for slot in range(slots)]

    def angles():
        lane = lax.broadcasted_iota(jnp.int32, (FRAME, HEAD_DIM), 1)
        in_t = lane < SECTIONS[0]
        for f in range(own_frames):
            frame = position * own_frames + f
            t = frame - clip_span(counts_ref, clips, longest, frame)[0]
            cosines.append(jnp.where(in_t, cos_t[t], cos_hw[...]))
            sines.append(jnp.where(in_t, sin_t[t], sin_hw[...]))

    def send(copy, slot):
        for d in range(1, group):
            target = to_member(d)

            @pl.when(head_of(target, slot) < heads)
            def _():
                copy(slot, d, member, target).start()

    own_weight = pltpu.make_async_copy(
        w_ref.at[:, pl.ds(pl.multiple_of(tp * columns, columns), columns)],
        w_all.at[tp],
        w_local,
    )

    def give_values(slot):
        send(v_copy, slot)

        @pl.when(have[slot])
        def _():
            v_stay(slot).start()

    def give_keys(slot):
        for head in range(slot * group, slot * group + sized(slot)):
            for f in range(own_frames):
                k_own[head, f] = rotated(k_in, f, head)
        send(k_copy, slot)

    def give_queries(slot):
        for head in range(slot * group, slot * group + sized(slot)):
            for f in range(own_frames):
                part = slice(f * FRAME, (f + 1) * FRAME)
                q_own[head, part, :] = rotated(q_in, f, head)
        send(q_copy, slot)

    give_values(0)
    for load in loads[:-1]:
        load.wait()
    angles()
    give_keys(0)
    loads[-1].wait()
    for slot in range(slots):
        if slot + 1 < slots:
            give_values(slot + 1)
        give_queries(slot)
        if slot + 1 < slots:
            give_keys(slot + 1)

    scale = HEAD_DIM**-0.5 * math.log2(math.e)

    def start_halos(slot, what):
        for d in range(1, reach + 1):
            for up in (True, False):

                @pl.when(exists(d, up))
                def _():
                    halo_copy(slot, what, d, up, False).start()

    def spread(slot):
        mine = head_of(member, slot)
        k_all[slot][own_rows(member)] = k_own[mine]
        q_all[slot, query_rows(member), :] = q_own[mine]
        for d in range(1, reach + 1):
            for up in (True, False):

                @pl.when(jnp.logical_not(exists(d, up)))
                def _():
                    n = halo_frames(d)
                    blank = halo + span * d if up else span - n - span * d + halo
                    for buffer in (k_all, v_all):
                        buffer[slot][blank : blank + n] = jnp.zeros(
                            (n, FRAME, HEAD_DIM), jnp.bfloat16
                        )

        v_stay(slot).wait()
        for d in range(1, group):
            v_copy(slot, d, from_member(d), member).wait_recv()
        start_halos(slot, 1)
        for d in range(1, group):
            k_copy(slot, d, from_member(d), member).wait_recv()
        start_halos(slot, 0)

    def settle(slot):
        for what in (1, 0):
            for d in range(1, reach + 1):
                for up in (True, False):

                    @pl.when(exists(d, not up))
                    def _():
                        halo_copy(slot, what, d, up, True).wait_recv()

    column = lax.broadcasted_iota(jnp.int32, (1, longest * FRAME), 1)

    def attend(slot, d, carry):
        target = from_member(d)

        @pl.when(d > 0)
        def _():
            q_copy(slot, d, target, member).wait_recv()

        for f in range(own_frames):
            place = target * own_frames + f
            start, stop = clip_span(counts_ref, clips, longest, first_frame + place)
            here = pl.ds(pl.multiple_of(place * FRAME, FRAME), FRAME)
            first_key = start - first_frame + halo
            queries = q_all[slot, here, :]
            keys = jnp.concatenate(
                [k_all[slot][first_key + i] for i in range(longest)], axis=0
            )
            values = jnp.concatenate(
                [v_all[slot][first_key + i] for i in range(longest)], axis=0
            )
            scores = lax.dot_general(
                queries, keys, (((1,), (1,)), ((), ())), preferred_element_type=jnp.float32
            )
            scores = jnp.where(column < (stop - start) * FRAME, scores, NEG_FILL)
            largest = jnp.max(scores, axis=1, keepdims=True)
            expo = jnp.exp2((scores - largest) * scale)
            total = jnp.sum(expo, axis=1, keepdims=True)
            summed = jnp.dot(
                expo.astype(jnp.bfloat16), values, preferred_element_type=jnp.float32
            )
            o_mine[slot, here, :] = (summed / total).astype(jnp.bfloat16)

        @pl.when(d > 0)
        def _():
            o_copy(slot, group - d, member, target).start()

        return carry

    def attend_some(slot, low, high):
        lax.fori_loop(low, high, functools.partial(attend, slot), 0)

    @pl.when(have[0])
    def _():
        spread(0)
        settle(0)
        attend_some(0, 0, 2)
        o_all[tp, head_of(member, 0)] = o_mine[0, query_rows(member), :]

    own_weight.start()
    for d in range(1, peers):
        w_copy(d).start()

    for slot in range(1, slots + 1):
        if slot < slots:

            @pl.when(have[slot])
            def _():
                spread(slot)

        @pl.when(have[slot - 1])
        def _():
            attend_some(slot - 1, 2, group)

        if slot < slots:

            @pl.when(have[slot])
            def _():
                settle(slot)
                attend_some(slot, 0, 2)
                o_all[tp, head_of(member, slot)] = o_mine[slot, query_rows(member), :]

    chunk = 256

    def project(source, slot, first, last):
        slot_heads = range(slot * group, slot * group + sized(slot))
        left = jnp.concatenate([o_all[source, head] for head in slot_heads], axis=1)
        deep = slice(slot * group * HEAD_DIM, (slot * group + sized(slot)) * HEAD_DIM)

        def body(step, carry):
            place = pl.ds(pl.multiple_of(step * chunk, chunk), chunk)
            term = jnp.dot(left, w_all[source, deep, place], preferred_element_type=jnp.float32)
            if not first:
                term = total_ref[:, place] + term
            if last:
                out_ref[:, place] = term.astype(jnp.bfloat16)
            else:
                total_ref[:, place] = term
            return carry

        lax.fori_loop(0, columns // chunk, body, 0)

    own_weight.wait()
    for slot in range(slots):
        for d in range(1, group):
            source = from_member(d)

            @pl.when(head_of(source, slot) < heads)
            def _():
                o_copy(slot, d, source, member).wait_recv()

        for d in range(1, peers):
            x_copy(slot, d, tp, lax.rem(tp + d, peers)).start()
        project(tp, slot, slot == 0, peers == 1 and slot == slots - 1)

    for d in range(1, peers):
        w_arrival(d).wait_recv()
    for slot in range(slots):
        for d in range(1, peers):
            source = lax.rem(tp - d + peers, peers)
            x_copy(slot, d, source, tp).wait_recv()
            project(source, slot, False, slot == slots - 1 and d == peers - 1)

    for d in range(1, peers):
        w_copy(d).wait_send()
    for slot in range(slots):
        for d in range(1, peers):
            x_copy(slot, d, tp, lax.rem(tp + d, peers)).wait_send()
        for d in range(1, group):
            target = to_member(d)

            @pl.when(head_of(target, slot) < heads)
            def _():
                k_copy(slot, d, member, target).wait_send()
                v_copy(slot, d, member, target).wait_send()
                q_copy(slot, d, member, target).wait_send()

            @pl.when(have[slot])
            def _():
                o_copy(slot, d, member, target).wait_send()

        for d in range(1, reach + 1):
            for up in (True, False):

                @pl.when(have[slot] & exists(d, up))
                def _():
                    for what in (0, 1):
                        halo_copy(slot, what, d, up, False).wait_send()


def per_device(seq, peers, query_rows, key_rows, value_rows, frame_counts, out_weight):
    rows, features = query_rows.shape
    heads = features // HEAD_DIM
    own_frames = rows // FRAME
    longest = own_frames * seq // 8
    group = 4
    groups = seq // group
    slots = -(-heads // group)
    columns = out_weight.shape[1] // peers
    clips = frame_counts.shape[0]
    span = group * own_frames
    halo = longest - 1
    reach = -(-halo // span)
    dims = (heads, group, groups, peers, slots, longest, clips, own_frames)
    value_frames = value_rows.reshape(own_frames, FRAME, features)
    vmem = pl.BlockSpec(memory_space=pltpu.VMEM)
    dma = pltpu.SemaphoreType.DMA
    bf16 = jnp.bfloat16
    flops = 2 * rows * features * out_weight.shape[1]
    return pl.pallas_call(
        functools.partial(kernel, dims),
        out_shape=jax.ShapeDtypeStruct((rows, columns), bf16),
        in_specs=[
            pl.BlockSpec(memory_space=pltpu.SMEM),
        ]
        + [pl.BlockSpec(memory_space=pl.ANY)] * 9,
        out_specs=vmem,
        scratch_shapes=[
            pltpu.VMEM((rows, features), bf16),
            pltpu.VMEM((rows, features), bf16),
            pltpu.VMEM((FRAME, HEAD_DIM), jnp.float32),
            pltpu.VMEM((FRAME, HEAD_DIM), jnp.float32),
            pltpu.VMEM((longest, 1, HEAD_DIM), jnp.float32),
            pltpu.VMEM((longest, 1, HEAD_DIM), jnp.float32),
            pltpu.VMEM((HEAD_DIM, HEAD_DIM), bf16),
            pltpu.VMEM((heads, rows, HEAD_DIM), bf16),
            pltpu.VMEM((heads, own_frames, FRAME, HEAD_DIM), bf16),
            pltpu.VMEM((slots, group * rows, HEAD_DIM), bf16),
            [pltpu.VMEM((span + 2 * halo, FRAME, HEAD_DIM), bf16)] * slots,
            [pltpu.VMEM((span + 2 * halo, FRAME, HEAD_DIM), bf16)] * slots,
            pltpu.VMEM((slots, group * rows, HEAD_DIM), bf16),
            pltpu.VMEM((peers, heads, rows, HEAD_DIM), bf16),
            pltpu.VMEM((peers, features, columns), bf16),
            pltpu.VMEM((rows, columns), jnp.float32),
            dma((7,)),
            dma(()),
            dma((slots,)),
            dma((peers,)),
            dma((peers,)),
            dma((slots, group)),
            dma((slots, group)),
            dma((slots, group)),
            dma((slots, group)),
            dma((slots, group)),
            dma((slots, group)),
            dma((slots, 2, 2 * reach)),
            dma((slots, 2, 2 * reach)),
            dma((slots, group)),
            dma((slots, group)),
            dma((slots, peers)),
            dma((slots, peers)),
        ],
        compiler_params=pltpu.CompilerParams(
            collective_id=0, has_side_effects=True, vmem_limit_bytes=56 * 1024 * 1024
        ),
        cost_estimate=pl.CostEstimate(flops=flops, bytes_accessed=8 << 20, transcendentals=0),
    )(frame_counts, query_rows, key_rows, value_frames, out_weight, *rope_tables(longest))


def solution(mesh):
    return jax.shard_map(
        functools.partial(per_device, mesh.shape["seq"], mesh.shape["tp"]),
        mesh=mesh,
        in_specs=(P("seq", "tp"), P("seq", "tp"), P("seq", "tp"), P(), P("tp", None)),
        out_specs=P("seq", "tp"),
        check_vma=False,
    )
```

```python
import functools
import math

import jax
import jax.numpy as jnp
import numpy as np
from jax import lax
from jax.experimental import pallas as pl
from jax.experimental.pallas import tpu as pltpu
from jax.sharding import PartitionSpec as P

SECTIONS = (16, 56, 56)
PH = 16
PW = 16
FRAME = PH * PW
HEAD_DIM = 128
ROPE_BASE = 256.0
NEG_FILL = -1e30
MESH = pl.DeviceIdType.MESH


def rope_tables(longest):
    angle_hw = np.zeros((FRAME, HEAD_DIM), np.float64)
    angle_t = np.zeros((longest, HEAD_DIM), np.float64)
    pairing = np.zeros((HEAD_DIM, HEAD_DIM), np.float32)
    row = np.arange(FRAME)
    first = 0
    for section, width in enumerate(SECTIONS):
        half = width // 2
        frequency = np.exp(-(2.0 * np.arange(half) / width) * math.log(ROPE_BASE))
        frequency = np.concatenate([frequency, frequency])
        lanes = slice(first, first + width)
        if section == 0:
            angle_t[:, lanes] = np.arange(longest)[:, None] * frequency[None, :]
        else:
            place = row // PW if section == 1 else row % PW
            angle_hw[:, lanes] = place[:, None] * frequency[None, :]
        for j in range(half):
            pairing[first + half + j, first + j] = -1.0
            pairing[first + j, first + half + j] = 1.0
        first += width
    angle_t = angle_t[:, None, :]
    tables = [np.cos(angle_hw), np.sin(angle_hw), np.cos(angle_t), np.sin(angle_t)]
    return [jnp.asarray(table, jnp.float32) for table in tables] + [
        jnp.asarray(pairing, jnp.bfloat16)
    ]


def clip_span(counts_ref, clips, longest, frame):
    start = jnp.int32(0)
    stop = jnp.int32(1 << 30)
    end = jnp.int32(0)
    for clip in range(clips):
        end = end + counts_ref[clip]
        start = jnp.where(end <= frame, end, start)
        stop = jnp.where(end > frame, jnp.minimum(stop, end), stop)
    return jnp.clip(start, frame - (longest - 1), frame), stop


def kernel(
    dims,
    counts_ref,
    q_ref,
    k_ref,
    v_ref,
    w_ref,
    cos_hw_ref,
    sin_hw_ref,
    cos_t_ref,
    sin_t_ref,
    pairing_ref,
    out_ref,
    q_in,
    k_in,
    cos_hw,
    sin_hw,
    cos_t,
    sin_t,
    pairing,
    q_own,
    k_own,
    q_all,
    k_all,
    v_all,
    o_mine,
    o_all,
    w_all,
    total_ref,
    in_local,
    w_local,
    v_local,
    w_send,
    w_recv,
    k_send,
    k_recv,
    v_send,
    v_recv,
    q_send,
    q_recv,
    halo_send,
    halo_recv,
    o_send,
    o_recv,
    x_send,
    x_recv,
):
    heads, group, groups, peers, slots, longest, clips, own_frames = dims
    rows = own_frames * FRAME
    halo = longest - 1
    span = group * own_frames
    reach = (halo + span - 1) // span
    columns = out_ref.shape[1]
    position = lax.axis_index("seq")
    tp = lax.axis_index("tp")
    plane = position // group
    member = position % group
    first_frame = plane * span

    def head_of(who, slot):
        return lax.rem(who - 2 * tp + 2 * group * peers, group) + slot * group

    def sized(slot):
        return min(group, heads - slot * group)

    def to_member(d):
        return lax.rem(member + d, group)

    def from_member(d):
        return lax.rem(member - d + group, group)

    def device(seq, core):
        return (seq, core)

    loads = [
        pltpu.make_async_copy(source, target, in_local.at[i])
        for i, (source, target) in enumerate(
            [
                (cos_hw_ref, cos_hw),
                (sin_hw_ref, sin_hw),
                (cos_t_ref, cos_t),
                (sin_t_ref, sin_t),
                (pairing_ref, pairing),
                (k_ref, k_in),
                (q_ref, q_in),
            ]
        )
    ]
    for load in loads:
        load.start()

    barrier = pltpu.get_barrier_semaphore()
    for d in range(1, group):
        pl.semaphore_signal(
            barrier, inc=1, device_id=device(plane * group + to_member(d), tp), device_id_type=MESH
        )
    for d in range(1, peers):
        pl.semaphore_signal(
            barrier, inc=1, device_id=device(position, lax.rem(tp + d, peers)), device_id_type=MESH
        )
    greeted = jnp.int32(group - 1 + peers - 1)
    for d in range(1, reach + 1):
        above = plane + d < groups
        below = plane - d >= 0

        @pl.when(above)
        def _():
            pl.semaphore_signal(
                barrier, inc=1, device_id=device(position + d * group, tp), device_id_type=MESH
            )

        @pl.when(below)
        def _():
            pl.semaphore_signal(
                barrier, inc=1, device_id=device(position - d * group, tp), device_id_type=MESH
            )

        greeted = greeted + above.astype(jnp.int32) + below.astype(jnp.int32)
    pl.semaphore_wait(barrier, greeted)

    cosines, sines = [], []

    def rotated(ref, f, head):
        x = ref[f * FRAME : (f + 1) * FRAME, head * HEAD_DIM : (head + 1) * HEAD_DIM]
        paired = jnp.dot(x, pairing[...], preferred_element_type=jnp.float32)
        return (x.astype(jnp.float32) * cosines[f] + paired * sines[f]).astype(jnp.bfloat16)

    def own_rows(who):
        return pl.ds(halo + who * own_frames, own_frames)

    def query_rows(who):
        return pl.ds(pl.multiple_of(who * rows, rows), rows)

    def lanes_of(head):
        return pl.ds(pl.multiple_of(head * HEAD_DIM, HEAD_DIM), HEAD_DIM)

    def k_copy(slot, d, source, target):
        return pltpu.make_async_remote_copy(
            src_ref=k_own.at[head_of(target, slot)],
            dst_ref=k_all[slot].at[own_rows(source)],
            send_sem=k_send.at[slot, d],
            recv_sem=k_recv.at[slot, d],
            device_id=device(plane * group + target, tp),
            device_id_type=MESH,
        )

    def v_copy(slot, d, source, target):
        return pltpu.make_async_remote_copy(
            src_ref=v_ref.at[:, :, lanes_of(head_of(target, slot))],
            dst_ref=v_all[slot].at[own_rows(source)],
            send_sem=v_send.at[slot, d],
            recv_sem=v_recv.at[slot, d],
            device_id=device(plane * group + target, tp),
            device_id_type=MESH,
        )

    def v_stay(slot):
        return pltpu.make_async_copy(
            v_ref.at[:, :, lanes_of(head_of(member, slot))],
            v_all[slot].at[own_rows(member)],
            v_local.at[slot],
        )

    def q_copy(slot, d, source, target):
        return pltpu.make_async_remote_copy(
            src_ref=q_own.at[head_of(target, slot)],
            dst_ref=q_all.at[slot, query_rows(source), :],
            send_sem=q_send.at[slot, d],
            recv_sem=q_recv.at[slot, d],
            device_id=device(plane * group + target, tp),
            device_id_type=MESH,
        )

    def o_copy(slot, d, source, target):
        return pltpu.make_async_remote_copy(
            src_ref=o_mine.at[slot, query_rows(target), :],
            dst_ref=o_all.at[tp, head_of(source, slot)],
            send_sem=o_send.at[slot, d],
            recv_sem=o_recv.at[slot, d],
            device_id=device(plane * group + target, tp),
            device_id_type=MESH,
        )

    def w_copy(d):
        target = lax.rem(tp + d, peers)
        return pltpu.make_async_remote_copy(
            src_ref=w_ref.at[:, pl.ds(pl.multiple_of(target * columns, columns), columns)],
            dst_ref=w_all.at[tp],
            send_sem=w_send.at[d],
            recv_sem=w_recv.at[d],
            device_id=device(position, target),
            device_id_type=MESH,
        )

    def w_arrival(d):
        source = lax.rem(tp - d + peers, peers)
        return pltpu.make_async_remote_copy(
            src_ref=w_ref.at[:, pl.ds(pl.multiple_of(tp * columns, columns), columns)],
            dst_ref=w_all.at[source],
            send_sem=w_send.at[d],
            recv_sem=w_recv.at[d],
            device_id=device(position, source),
            device_id_type=MESH,
        )

    def x_copy(slot, d, source, target):
        span_heads = pl.ds(slot * group, sized(slot))
        return pltpu.make_async_remote_copy(
            src_ref=o_all.at[source, span_heads],
            dst_ref=o_all.at[source, span_heads],
            send_sem=x_send.at[slot, d],
            recv_sem=x_recv.at[slot, d],
            device_id=device(position, target),
            device_id_type=MESH,
        )

    def halo_frames(d):
        return min(span, halo - span * (d - 1))

    def halo_copy(slot, what, d, upward, arriving):
        n = halo_frames(d)
        if upward:
            src_frame, dst_frame = halo + span - n, span - n - span * d + halo
        else:
            src_frame, dst_frame = halo, halo + span * d
        which = 2 * (d - 1) + (0 if upward else 1)
        away = d * group if upward != arriving else -d * group
        buffer = (k_all, v_all)[what][slot]
        return pltpu.make_async_remote_copy(
            src_ref=buffer.at[pl.ds(src_frame, n)],
            dst_ref=buffer.at[pl.ds(dst_frame, n)],
            send_sem=halo_send.at[slot, what, which],
            recv_sem=halo_recv.at[slot, what, which],
            device_id=device(position + away, tp),
            device_id_type=MESH,
        )

    def exists(d, up):
        return plane + d < groups if up else plane - d >= 0

    have = [head_of(member, slot) < heads for slot in range(slots)]

    def angles():
        lane = lax.broadcasted_iota(jnp.int32, (FRAME, HEAD_DIM), 1)
        in_t = lane < SECTIONS[0]
        for f in range(own_frames):
            frame = position * own_frames + f
            t = frame - clip_span(counts_ref, clips, longest, frame)[0]
            cosines.append(jnp.where(in_t, cos_t[t], cos_hw[...]))
            sines.append(jnp.where(in_t, sin_t[t], sin_hw[...]))

    def send(copy, slot):
        for d in range(1, group):
            target = to_member(d)

            @pl.when(head_of(target, slot) < heads)
            def _():
                copy(slot, d, member, target).start()

    own_weight = pltpu.make_async_copy(
        w_ref.at[:, pl.ds(pl.multiple_of(tp * columns, columns), columns)],
        w_all.at[tp],
        w_local,
    )

    def give_values(slot):
        send(v_copy, slot)

        @pl.when(have[slot])
        def _():
            v_stay(slot).start()

    def give_keys(slot):
        for head in range(slot * group, slot * group + sized(slot)):
            for f in range(own_frames):
                k_own[head, f] = rotated(k_in, f, head)
        send(k_copy, slot)

    def give_queries(slot):
        for head in range(slot * group, slot * group + sized(slot)):
            for f in range(own_frames):
                part = slice(f * FRAME, (f + 1) * FRAME)
                q_own[head, part, :] = rotated(q_in, f, head)
        send(q_copy, slot)

    give_values(0)
    for load in loads[:-1]:
        load.wait()
    angles()
    give_keys(0)
    loads[-1].wait()
    for slot in range(slots):
        if slot + 1 < slots:
            give_values(slot + 1)
        give_queries(slot)
        if slot + 1 < slots:
            give_keys(slot + 1)

    scale = HEAD_DIM**-0.5 * math.log2(math.e)

    def start_halos(slot, what):
        for d in range(1, reach + 1):
            for up in (True, False):

                @pl.when(exists(d, up))
                def _():
                    halo_copy(slot, what, d, up, False).start()

    def spread(slot):
        mine = head_of(member, slot)
        k_all[slot][own_rows(member)] = k_own[mine]
        q_all[slot, query_rows(member), :] = q_own[mine]
        for d in range(1, reach + 1):
            for up in (True, False):

                @pl.when(jnp.logical_not(exists(d, up)))
                def _():
                    n = halo_frames(d)
                    blank = halo + span * d if up else span - n - span * d + halo
                    for buffer in (k_all, v_all):
                        buffer[slot][blank : blank + n] = jnp.zeros(
                            (n, FRAME, HEAD_DIM), jnp.bfloat16
                        )

        v_stay(slot).wait()
        for d in range(1, group):
            v_copy(slot, d, from_member(d), member).wait_recv()
        start_halos(slot, 1)
        for d in range(1, group):
            k_copy(slot, d, from_member(d), member).wait_recv()
        start_halos(slot, 0)

    def settle(slot):
        for what in (1, 0):
            for d in range(1, reach + 1):
                for up in (True, False):

                    @pl.when(exists(d, not up))
                    def _():
                        halo_copy(slot, what, d, up, True).wait_recv()

    column = lax.broadcasted_iota(jnp.int32, (1, longest * FRAME), 1)

    def attend(slot, d, carry):
        target = from_member(d)

        @pl.when(d > 0)
        def _():
            q_copy(slot, d, target, member).wait_recv()

        for f in range(own_frames):
            place = target * own_frames + f
            start, stop = clip_span(counts_ref, clips, longest, first_frame + place)
            here = pl.ds(pl.multiple_of(place * FRAME, FRAME), FRAME)
            first_key = start - first_frame + halo
            queries = q_all[slot, here, :]
            keys = jnp.concatenate(
                [k_all[slot][first_key + i] for i in range(longest)], axis=0
            )
            values = jnp.concatenate(
                [v_all[slot][first_key + i] for i in range(longest)], axis=0
            )
            scores = lax.dot_general(
                queries, keys, (((1,), (1,)), ((), ())), preferred_element_type=jnp.float32
            )
            scores = jnp.where(column < (stop - start) * FRAME, scores, NEG_FILL)
            largest = jnp.max(scores, axis=1, keepdims=True)
            expo = jnp.exp2((scores - largest) * scale)
            total = jnp.sum(expo, axis=1, keepdims=True)
            summed = jnp.dot(
                expo.astype(jnp.bfloat16), values, preferred_element_type=jnp.float32
            )
            o_mine[slot, here, :] = (summed / total).astype(jnp.bfloat16)

        @pl.when(d > 0)
        def _():
            o_copy(slot, group - d, member, target).start()

        return carry

    def attend_some(slot, low, high):
        lax.fori_loop(low, high, functools.partial(attend, slot), 0)

    @pl.when(have[0])
    def _():
        spread(0)
        settle(0)
        attend_some(0, 0, 2)
        o_all[tp, head_of(member, 0)] = o_mine[0, query_rows(member), :]

    own_weight.start()
    for d in range(1, peers):
        w_copy(d).start()

    for slot in range(1, slots + 1):
        if slot < slots:

            @pl.when(have[slot])
            def _():
                spread(slot)

        @pl.when(have[slot - 1])
        def _():
            attend_some(slot - 1, 2, group)

        if slot < slots:

            @pl.when(have[slot])
            def _():
                settle(slot)
                attend_some(slot, 0, 2)
                o_all[tp, head_of(member, slot)] = o_mine[slot, query_rows(member), :]

    chunk = 256

    def project(source, slot, first, last):
        slot_heads = range(slot * group, slot * group + sized(slot))
        left = jnp.concatenate([o_all[source, head] for head in slot_heads], axis=1)
        deep = slice(slot * group * HEAD_DIM, (slot * group + sized(slot)) * HEAD_DIM)

        def body(step, carry):
            place = pl.ds(pl.multiple_of(step * chunk, chunk), chunk)
            term = jnp.dot(left, w_all[source, deep, place], preferred_element_type=jnp.float32)
            if not first:
                term = total_ref[:, place] + term
            if last:
                out_ref[:, place] = term.astype(jnp.bfloat16)
            else:
                total_ref[:, place] = term
            return carry

        lax.fori_loop(0, columns // chunk, body, 0)

    own_weight.wait()
    for slot in range(slots):
        for d in range(1, group):
            source = from_member(d)

            @pl.when(head_of(source, slot) < heads)
            def _():
                o_copy(slot, d, source, member).wait_recv()

        for d in range(1, peers):
            x_copy(slot, d, tp, lax.rem(tp + d, peers)).start()
        project(tp, slot, slot == 0, peers == 1 and slot == slots - 1)

    for d in range(1, peers):
        w_arrival(d).wait_recv()
    for slot in range(slots):
        for d in range(1, peers):
            source = lax.rem(tp - d + peers, peers)
            x_copy(slot, d, source, tp).wait_recv()
            project(source, slot, False, slot == slots - 1 and d == peers - 1)

    for d in range(1, peers):
        w_copy(d).wait_send()
    for slot in range(slots):
        for d in range(1, peers):
            x_copy(slot, d, tp, lax.rem(tp + d, peers)).wait_send()
        for d in range(1, group):
            target = to_member(d)

            @pl.when(head_of(target, slot) < heads)
            def _():
                k_copy(slot, d, member, target).wait_send()
                v_copy(slot, d, member, target).wait_send()
                q_copy(slot, d, member, target).wait_send()

            @pl.when(have[slot])
            def _():
                o_copy(slot, d, member, target).wait_send()

        for d in range(1, reach + 1):
            for up in (True, False):

                @pl.when(have[slot] & exists(d, up))
                def _():
                    for what in (0, 1):
                        halo_copy(slot, what, d, up, False).wait_send()


def hand_over(pieces, from_ref, to_ref, done):
    rows = from_ref.shape[0] // pieces
    copies = [
        pltpu.make_async_copy(
            from_ref.at[pl.ds(i * rows, rows)], to_ref.at[pl.ds(i * rows, rows)], done.at[i]
        )
        for i in range(pieces)
    ]
    for copy in copies:
        copy.start()
    for copy in copies:
        copy.wait()


def per_device(seq, peers, query_rows, key_rows, value_rows, frame_counts, out_weight):
    rows, features = query_rows.shape
    heads = features // HEAD_DIM
    own_frames = rows // FRAME
    longest = own_frames * seq // 8
    group = 4
    groups = seq // group
    slots = -(-heads // group)
    columns = out_weight.shape[1] // peers
    clips = frame_counts.shape[0]
    span = group * own_frames
    halo = longest - 1
    reach = -(-halo // span)
    dims = (heads, group, groups, peers, slots, longest, clips, own_frames)
    value_frames = value_rows.reshape(own_frames, FRAME, features)
    vmem = pl.BlockSpec(memory_space=pltpu.VMEM)
    dma = pltpu.SemaphoreType.DMA
    bf16 = jnp.bfloat16
    flops = 2 * rows * features * out_weight.shape[1]
    mixed = pl.pallas_call(
        functools.partial(kernel, dims),
        out_shape=jax.ShapeDtypeStruct((rows, columns), bf16),
        in_specs=[
            pl.BlockSpec(memory_space=pltpu.SMEM),
        ]
        + [pl.BlockSpec(memory_space=pl.ANY)] * 9,
        out_specs=vmem,
        scratch_shapes=[
            pltpu.VMEM((rows, features), bf16),
            pltpu.VMEM((rows, features), bf16),
            pltpu.VMEM((FRAME, HEAD_DIM), jnp.float32),
            pltpu.VMEM((FRAME, HEAD_DIM), jnp.float32),
            pltpu.VMEM((longest, 1, HEAD_DIM), jnp.float32),
            pltpu.VMEM((longest, 1, HEAD_DIM), jnp.float32),
            pltpu.VMEM((HEAD_DIM, HEAD_DIM), bf16),
            pltpu.VMEM((heads, rows, HEAD_DIM), bf16),
            pltpu.VMEM((heads, own_frames, FRAME, HEAD_DIM), bf16),
            pltpu.VMEM((slots, group * rows, HEAD_DIM), bf16),
            [pltpu.VMEM((span + 2 * halo, FRAME, HEAD_DIM), bf16)] * slots,
            [pltpu.VMEM((span + 2 * halo, FRAME, HEAD_DIM), bf16)] * slots,
            pltpu.VMEM((slots, group * rows, HEAD_DIM), bf16),
            pltpu.VMEM((peers, heads, rows, HEAD_DIM), bf16),
            pltpu.VMEM((peers, features, columns), bf16),
            pltpu.VMEM((rows, columns), jnp.float32),
            dma((7,)),
            dma(()),
            dma((slots,)),
            dma((peers,)),
            dma((peers,)),
            dma((slots, group)),
            dma((slots, group)),
            dma((slots, group)),
            dma((slots, group)),
            dma((slots, group)),
            dma((slots, group)),
            dma((slots, 2, 2 * reach)),
            dma((slots, 2, 2 * reach)),
            dma((slots, group)),
            dma((slots, group)),
            dma((slots, peers)),
            dma((slots, peers)),
        ],
        compiler_params=pltpu.CompilerParams(
            collective_id=0, has_side_effects=True, vmem_limit_bytes=56 * 1024 * 1024
        ),
        cost_estimate=pl.CostEstimate(flops=flops, bytes_accessed=8 << 20, transcendentals=0),
    )(frame_counts, query_rows, key_rows, value_frames, out_weight, *rope_tables(longest))
    pieces = 8
    return pl.pallas_call(
        functools.partial(hand_over, pieces),
        out_shape=jax.ShapeDtypeStruct((rows, columns), bf16),
        in_specs=[pl.BlockSpec(memory_space=pl.ANY)],
        out_specs=pl.BlockSpec(memory_space=pl.ANY),
        scratch_shapes=[dma((pieces,))],
        compiler_params=pltpu.CompilerParams(vmem_limit_bytes=56 * 1024 * 1024),
        cost_estimate=pl.CostEstimate(flops=0, bytes_accessed=4 << 20, transcendentals=0),
    )(mixed)


def solution(mesh):
    return jax.shard_map(
        functools.partial(per_device, mesh.shape["seq"], mesh.shape["tp"]),
        mesh=mesh,
        in_specs=(P("seq", "tp"), P("seq", "tp"), P("seq", "tp"), P(), P("tp", None)),
        out_specs=P("seq", "tp"),
        check_vma=False,
    )
```

```python
import functools
import math

import jax
import jax.numpy as jnp
import numpy as np
from jax import lax
from jax.experimental import pallas as pl
from jax.experimental.pallas import tpu as pltpu
from jax.sharding import PartitionSpec as P

SECTIONS = (16, 56, 56)
PH = 16
PW = 16
FRAME = PH * PW
HEAD_DIM = 128
ROPE_BASE = 256.0
NEG_FILL = -1e30
MESH = pl.DeviceIdType.MESH


def rope_tables(longest):
    angle_hw = np.zeros((FRAME, HEAD_DIM), np.float64)
    angle_t = np.zeros((longest, HEAD_DIM), np.float64)
    pairing = np.zeros((HEAD_DIM, HEAD_DIM), np.float32)
    row = np.arange(FRAME)
    first = 0
    for section, width in enumerate(SECTIONS):
        half = width // 2
        frequency = np.exp(-(2.0 * np.arange(half) / width) * math.log(ROPE_BASE))
        frequency = np.concatenate([frequency, frequency])
        lanes = slice(first, first + width)
        if section == 0:
            angle_t[:, lanes] = np.arange(longest)[:, None] * frequency[None, :]
        else:
            place = row // PW if section == 1 else row % PW
            angle_hw[:, lanes] = place[:, None] * frequency[None, :]
        for j in range(half):
            pairing[first + half + j, first + j] = -1.0
            pairing[first + j, first + half + j] = 1.0
        first += width
    angle_t = angle_t[:, None, :]
    tables = [np.cos(angle_hw), np.sin(angle_hw), np.cos(angle_t), np.sin(angle_t)]
    return [jnp.asarray(table, jnp.float32) for table in tables] + [
        jnp.asarray(pairing, jnp.bfloat16)
    ]


def clip_span(counts_ref, clips, longest, frame):
    start = jnp.int32(0)
    stop = jnp.int32(1 << 30)
    end = jnp.int32(0)
    for clip in range(clips):
        end = end + counts_ref[clip]
        start = jnp.where(end <= frame, end, start)
        stop = jnp.where(end > frame, jnp.minimum(stop, end), stop)
    return jnp.clip(start, frame - (longest - 1), frame), stop


def kernel(
    dims,
    counts_ref,
    q_ref,
    k_ref,
    v_ref,
    w_ref,
    cos_hw_ref,
    sin_hw_ref,
    cos_t_ref,
    sin_t_ref,
    pairing_ref,
    out_ref,
    q_in,
    k_in,
    cos_hw,
    sin_hw,
    cos_t,
    sin_t,
    pairing,
    q_own,
    k_own,
    q_all,
    k_all,
    v_all,
    o_mine,
    o_all,
    w_all,
    total_ref,
    in_local,
    w_local,
    v_local,
    w_send,
    w_recv,
    k_send,
    k_recv,
    v_send,
    v_recv,
    q_send,
    q_recv,
    halo_send,
    halo_recv,
    o_send,
    o_recv,
    x_send,
    x_recv,
):
    heads, group, groups, peers, slots, longest, clips, own_frames = dims
    rows = own_frames * FRAME
    halo = longest - 1
    span = group * own_frames
    reach = (halo + span - 1) // span
    columns = out_ref.shape[1]
    position = lax.axis_index("seq")
    tp = lax.axis_index("tp")
    plane = position // group
    member = position % group
    first_frame = plane * span

    def head_of(who, slot):
        return lax.rem(who - 2 * tp + 2 * group * peers, group) + slot * group

    def sized(slot):
        return min(group, heads - slot * group)

    def to_member(d):
        return lax.rem(member + d, group)

    def from_member(d):
        return lax.rem(member - d + group, group)

    def device(seq, core):
        return (seq, core)

    loads = [
        pltpu.make_async_copy(source, target, in_local.at[i])
        for i, (source, target) in enumerate(
            [
                (cos_hw_ref, cos_hw),
                (sin_hw_ref, sin_hw),
                (cos_t_ref, cos_t),
                (sin_t_ref, sin_t),
                (pairing_ref, pairing),
                (k_ref, k_in),
                (q_ref, q_in),
            ]
        )
    ]
    for load in loads:
        load.start()

    barrier = pltpu.get_barrier_semaphore()
    for d in range(1, group):
        pl.semaphore_signal(
            barrier, inc=1, device_id=device(plane * group + to_member(d), tp), device_id_type=MESH
        )
    for d in range(1, peers):
        pl.semaphore_signal(
            barrier, inc=1, device_id=device(position, lax.rem(tp + d, peers)), device_id_type=MESH
        )
    greeted = jnp.int32(group - 1 + peers - 1)
    for d in range(1, reach + 1):
        above = plane + d < groups
        below = plane - d >= 0

        @pl.when(above)
        def _():
            pl.semaphore_signal(
                barrier, inc=1, device_id=device(position + d * group, tp), device_id_type=MESH
            )

        @pl.when(below)
        def _():
            pl.semaphore_signal(
                barrier, inc=1, device_id=device(position - d * group, tp), device_id_type=MESH
            )

        greeted = greeted + above.astype(jnp.int32) + below.astype(jnp.int32)
    pl.semaphore_wait(barrier, greeted)

    cosines, sines = [], []

    def rotated(ref, f, head):
        x = ref[f * FRAME : (f + 1) * FRAME, head * HEAD_DIM : (head + 1) * HEAD_DIM]
        paired = jnp.dot(x, pairing[...], preferred_element_type=jnp.float32)
        return (x.astype(jnp.float32) * cosines[f] + paired * sines[f]).astype(jnp.bfloat16)

    def own_rows(who):
        return pl.ds(halo + who * own_frames, own_frames)

    def query_rows(who):
        return pl.ds(pl.multiple_of(who * rows, rows), rows)

    def lanes_of(head):
        return pl.ds(pl.multiple_of(head * HEAD_DIM, HEAD_DIM), HEAD_DIM)

    def k_copy(slot, d, source, target):
        return pltpu.make_async_remote_copy(
            src_ref=k_own.at[head_of(target, slot)],
            dst_ref=k_all[slot].at[own_rows(source)],
            send_sem=k_send.at[slot, d],
            recv_sem=k_recv.at[slot, d],
            device_id=device(plane * group + target, tp),
            device_id_type=MESH,
        )

    def v_copy(slot, d, source, target):
        return pltpu.make_async_remote_copy(
            src_ref=v_ref.at[:, :, lanes_of(head_of(target, slot))],
            dst_ref=v_all[slot].at[own_rows(source)],
            send_sem=v_send.at[slot, d],
            recv_sem=v_recv.at[slot, d],
            device_id=device(plane * group + target, tp),
            device_id_type=MESH,
        )

    def v_stay(slot):
        return pltpu.make_async_copy(
            v_ref.at[:, :, lanes_of(head_of(member, slot))],
            v_all[slot].at[own_rows(member)],
            v_local.at[slot],
        )

    def q_copy(slot, d, source, target):
        return pltpu.make_async_remote_copy(
            src_ref=q_own.at[head_of(target, slot)],
            dst_ref=q_all.at[slot, query_rows(source), :],
            send_sem=q_send.at[slot, d],
            recv_sem=q_recv.at[slot, d],
            device_id=device(plane * group + target, tp),
            device_id_type=MESH,
        )

    def o_copy(slot, d, source, target):
        return pltpu.make_async_remote_copy(
            src_ref=o_mine.at[slot, query_rows(target), :],
            dst_ref=o_all.at[tp, head_of(source, slot)],
            send_sem=o_send.at[slot, d],
            recv_sem=o_recv.at[slot, d],
            device_id=device(plane * group + target, tp),
            device_id_type=MESH,
        )

    def w_copy(d):
        target = lax.rem(tp + d, peers)
        return pltpu.make_async_remote_copy(
            src_ref=w_ref.at[:, pl.ds(pl.multiple_of(target * columns, columns), columns)],
            dst_ref=w_all.at[tp],
            send_sem=w_send.at[d],
            recv_sem=w_recv.at[d],
            device_id=device(position, target),
            device_id_type=MESH,
        )

    def w_arrival(d):
        source = lax.rem(tp - d + peers, peers)
        return pltpu.make_async_remote_copy(
            src_ref=w_ref.at[:, pl.ds(pl.multiple_of(tp * columns, columns), columns)],
            dst_ref=w_all.at[source],
            send_sem=w_send.at[d],
            recv_sem=w_recv.at[d],
            device_id=device(position, source),
            device_id_type=MESH,
        )

    def x_copy(slot, d, source, target):
        span_heads = pl.ds(slot * group, sized(slot))
        return pltpu.make_async_remote_copy(
            src_ref=o_all.at[source, span_heads],
            dst_ref=o_all.at[source, span_heads],
            send_sem=x_send.at[slot, d],
            recv_sem=x_recv.at[slot, d],
            device_id=device(position, target),
            device_id_type=MESH,
        )

    def halo_frames(d):
        return min(span, halo - span * (d - 1))

    def halo_copy(slot, what, d, upward, arriving):
        n = halo_frames(d)
        if upward:
            src_frame, dst_frame = halo + span - n, span - n - span * d + halo
        else:
            src_frame, dst_frame = halo, halo + span * d
        which = 2 * (d - 1) + (0 if upward else 1)
        away = d * group if upward != arriving else -d * group
        buffer = (k_all, v_all)[what][slot]
        return pltpu.make_async_remote_copy(
            src_ref=buffer.at[pl.ds(src_frame, n)],
            dst_ref=buffer.at[pl.ds(dst_frame, n)],
            send_sem=halo_send.at[slot, what, which],
            recv_sem=halo_recv.at[slot, what, which],
            device_id=device(position + away, tp),
            device_id_type=MESH,
        )

    def exists(d, up):
        return plane + d < groups if up else plane - d >= 0

    have = [head_of(member, slot) < heads for slot in range(slots)]

    def angles():
        lane = lax.broadcasted_iota(jnp.int32, (FRAME, HEAD_DIM), 1)
        in_t = lane < SECTIONS[0]
        for f in range(own_frames):
            frame = position * own_frames + f
            t = frame - clip_span(counts_ref, clips, longest, frame)[0]
            cosines.append(jnp.where(in_t, cos_t[t], cos_hw[...]))
            sines.append(jnp.where(in_t, sin_t[t], sin_hw[...]))

    def send(copy, slot):
        for d in range(1, group):
            target = to_member(d)

            @pl.when(head_of(target, slot) < heads)
            def _():
                copy(slot, d, member, target).start()

    own_weight = pltpu.make_async_copy(
        w_ref.at[:, pl.ds(pl.multiple_of(tp * columns, columns), columns)],
        w_all.at[tp],
        w_local,
    )

    def give_values(slot):
        send(v_copy, slot)

        @pl.when(have[slot])
        def _():
            v_stay(slot).start()

    def give_keys(slot):
        for head in range(slot * group, slot * group + sized(slot)):
            for f in range(own_frames):
                k_own[head, f] = rotated(k_in, f, head)
        send(k_copy, slot)

    def give_queries(slot):
        for head in range(slot * group, slot * group + sized(slot)):
            for f in range(own_frames):
                part = slice(f * FRAME, (f + 1) * FRAME)
                q_own[head, part, :] = rotated(q_in, f, head)
        send(q_copy, slot)

    give_values(0)
    for load in loads[:-1]:
        load.wait()
    angles()
    give_keys(0)
    loads[-1].wait()
    for slot in range(slots):
        if slot + 1 < slots:
            give_values(slot + 1)
        give_queries(slot)
        if slot + 1 < slots:
            give_keys(slot + 1)

    scale = HEAD_DIM**-0.5 * math.log2(math.e)

    def start_halos(slot, what):
        for d in range(1, reach + 1):
            for up in (True, False):

                @pl.when(exists(d, up))
                def _():
                    halo_copy(slot, what, d, up, False).start()

    def spread(slot):
        mine = head_of(member, slot)
        k_all[slot][own_rows(member)] = k_own[mine]
        q_all[slot, query_rows(member), :] = q_own[mine]
        for d in range(1, reach + 1):
            for up in (True, False):

                @pl.when(jnp.logical_not(exists(d, up)))
                def _():
                    n = halo_frames(d)
                    blank = halo + span * d if up else span - n - span * d + halo
                    for buffer in (k_all, v_all):
                        buffer[slot][blank : blank + n] = jnp.zeros(
                            (n, FRAME, HEAD_DIM), jnp.bfloat16
                        )

        v_stay(slot).wait()
        for d in range(1, group):
            v_copy(slot, d, from_member(d), member).wait_recv()
        start_halos(slot, 1)
        for d in range(1, group):
            k_copy(slot, d, from_member(d), member).wait_recv()
        start_halos(slot, 0)

    def settle(slot):
        for what in (1, 0):
            for d in range(1, reach + 1):
                for up in (True, False):

                    @pl.when(exists(d, not up))
                    def _():
                        halo_copy(slot, what, d, up, True).wait_recv()

    column = lax.broadcasted_iota(jnp.int32, (1, longest * FRAME), 1)

    def attend(slot, d, carry):
        target = from_member(d)

        @pl.when(d > 0)
        def _():
            q_copy(slot, d, target, member).wait_recv()

        for f in range(own_frames):
            place = target * own_frames + f
            start, stop = clip_span(counts_ref, clips, longest, first_frame + place)
            here = pl.ds(pl.multiple_of(place * FRAME, FRAME), FRAME)
            first_key = start - first_frame + halo
            queries = q_all[slot, here, :]
            keys = jnp.concatenate(
                [k_all[slot][first_key + i] for i in range(longest)], axis=0
            )
            values = jnp.concatenate(
                [v_all[slot][first_key + i] for i in range(longest)], axis=0
            )
            scores = lax.dot_general(
                queries, keys, (((1,), (1,)), ((), ())), preferred_element_type=jnp.float32
            )
            scores = jnp.where(column < (stop - start) * FRAME, scores, NEG_FILL)
            largest = jnp.max(scores, axis=1, keepdims=True)
            expo = jnp.exp2((scores - largest) * scale)
            total = jnp.sum(expo, axis=1, keepdims=True)
            summed = jnp.dot(
                expo.astype(jnp.bfloat16), values, preferred_element_type=jnp.float32
            )
            o_mine[slot, here, :] = (summed / total).astype(jnp.bfloat16)

        @pl.when(d > 0)
        def _():
            o_copy(slot, group - d, member, target).start()

        return carry

    def attend_some(slot, low, high):
        lax.fori_loop(low, high, functools.partial(attend, slot), 0)

    @pl.when(have[0])
    def _():
        spread(0)
        settle(0)
        attend_some(0, 0, 2)
        o_all[tp, head_of(member, 0)] = o_mine[0, query_rows(member), :]

    own_weight.start()
    for d in range(1, peers):
        w_copy(d).start()

    for slot in range(1, slots + 1):
        if slot < slots:

            @pl.when(have[slot])
            def _():
                spread(slot)

        @pl.when(have[slot - 1])
        def _():
            attend_some(slot - 1, 2, group)

        if slot < slots:

            @pl.when(have[slot])
            def _():
                settle(slot)
                attend_some(slot, 0, 2)
                o_all[tp, head_of(member, slot)] = o_mine[slot, query_rows(member), :]

    chunk = 256

    def project(source, slot, first, last):
        slot_heads = range(slot * group, slot * group + sized(slot))
        left = jnp.concatenate([o_all[source, head] for head in slot_heads], axis=1)
        deep = slice(slot * group * HEAD_DIM, (slot * group + sized(slot)) * HEAD_DIM)

        def body(step, carry):
            place = pl.ds(pl.multiple_of(step * chunk, chunk), chunk)
            term = jnp.dot(left, w_all[source, deep, place], preferred_element_type=jnp.float32)
            if not first:
                term = total_ref[:, place] + term
            if last:
                out_ref[:, place] = term.astype(jnp.bfloat16)
            else:
                total_ref[:, place] = term
            return carry

        lax.fori_loop(0, columns // chunk, body, 0)

    own_weight.wait()
    for slot in range(slots):
        for d in range(1, group):
            source = from_member(d)

            @pl.when(head_of(source, slot) < heads)
            def _():
                o_copy(slot, d, source, member).wait_recv()

        for d in range(1, peers):
            x_copy(slot, d, tp, lax.rem(tp + d, peers)).start()
        project(tp, slot, slot == 0, peers == 1 and slot == slots - 1)

    for d in range(1, peers):
        w_arrival(d).wait_recv()
    for slot in range(slots):
        for d in range(1, peers):
            source = lax.rem(tp - d + peers, peers)
            x_copy(slot, d, source, tp).wait_recv()
            project(source, slot, False, slot == slots - 1 and d == peers - 1)

    for d in range(1, peers):
        w_copy(d).wait_send()
    for slot in range(slots):
        for d in range(1, peers):
            x_copy(slot, d, tp, lax.rem(tp + d, peers)).wait_send()
        for d in range(1, group):
            target = to_member(d)

            @pl.when(head_of(target, slot) < heads)
            def _():
                k_copy(slot, d, member, target).wait_send()
                v_copy(slot, d, member, target).wait_send()
                q_copy(slot, d, member, target).wait_send()

            @pl.when(have[slot])
            def _():
                o_copy(slot, d, member, target).wait_send()

        for d in range(1, reach + 1):
            for up in (True, False):

                @pl.when(have[slot] & exists(d, up))
                def _():
                    for what in (0, 1):
                        halo_copy(slot, what, d, up, False).wait_send()


def hand_over(from_ref, to_ref):
    to_ref[...] = from_ref[...]


def per_device(seq, peers, query_rows, key_rows, value_rows, frame_counts, out_weight):
    rows, features = query_rows.shape
    heads = features // HEAD_DIM
    own_frames = rows // FRAME
    longest = own_frames * seq // 8
    group = 4
    groups = seq // group
    slots = -(-heads // group)
    columns = out_weight.shape[1] // peers
    clips = frame_counts.shape[0]
    span = group * own_frames
    halo = longest - 1
    reach = -(-halo // span)
    dims = (heads, group, groups, peers, slots, longest, clips, own_frames)
    value_frames = value_rows.reshape(own_frames, FRAME, features)
    vmem = pl.BlockSpec(memory_space=pltpu.VMEM)
    dma = pltpu.SemaphoreType.DMA
    bf16 = jnp.bfloat16
    flops = 2 * rows * features * out_weight.shape[1]
    mixed = pl.pallas_call(
        functools.partial(kernel, dims),
        out_shape=jax.ShapeDtypeStruct((rows, columns), bf16),
        in_specs=[
            pl.BlockSpec(memory_space=pltpu.SMEM),
        ]
        + [pl.BlockSpec(memory_space=pl.ANY)] * 9,
        out_specs=vmem,
        scratch_shapes=[
            pltpu.VMEM((rows, features), bf16),
            pltpu.VMEM((rows, features), bf16),
            pltpu.VMEM((FRAME, HEAD_DIM), jnp.float32),
            pltpu.VMEM((FRAME, HEAD_DIM), jnp.float32),
            pltpu.VMEM((longest, 1, HEAD_DIM), jnp.float32),
            pltpu.VMEM((longest, 1, HEAD_DIM), jnp.float32),
            pltpu.VMEM((HEAD_DIM, HEAD_DIM), bf16),
            pltpu.VMEM((heads, rows, HEAD_DIM), bf16),
            pltpu.VMEM((heads, own_frames, FRAME, HEAD_DIM), bf16),
            pltpu.VMEM((slots, group * rows, HEAD_DIM), bf16),
            [pltpu.VMEM((span + 2 * halo, FRAME, HEAD_DIM), bf16)] * slots,
            [pltpu.VMEM((span + 2 * halo, FRAME, HEAD_DIM), bf16)] * slots,
            pltpu.VMEM((slots, group * rows, HEAD_DIM), bf16),
            pltpu.VMEM((peers, heads, rows, HEAD_DIM), bf16),
            pltpu.VMEM((peers, features, columns), bf16),
            pltpu.VMEM((rows, columns), jnp.float32),
            dma((7,)),
            dma(()),
            dma((slots,)),
            dma((peers,)),
            dma((peers,)),
            dma((slots, group)),
            dma((slots, group)),
            dma((slots, group)),
            dma((slots, group)),
            dma((slots, group)),
            dma((slots, group)),
            dma((slots, 2, 2 * reach)),
            dma((slots, 2, 2 * reach)),
            dma((slots, group)),
            dma((slots, group)),
            dma((slots, peers)),
            dma((slots, peers)),
        ],
        compiler_params=pltpu.CompilerParams(
            collective_id=0, has_side_effects=True, vmem_limit_bytes=56 * 1024 * 1024
        ),
        cost_estimate=pl.CostEstimate(flops=flops, bytes_accessed=8 << 20, transcendentals=0),
    )(frame_counts, query_rows, key_rows, value_frames, out_weight, *rope_tables(longest))
    block = pl.BlockSpec((rows // 4, columns), lambda i: (i, 0))
    return pl.pallas_call(
        hand_over,
        grid=(4,),
        out_shape=jax.ShapeDtypeStruct((rows, columns), bf16),
        in_specs=[block],
        out_specs=block,
        compiler_params=pltpu.CompilerParams(vmem_limit_bytes=56 * 1024 * 1024),
    )(mixed)


def solution(mesh):
    return jax.shard_map(
        functools.partial(per_device, mesh.shape["seq"], mesh.shape["tp"]),
        mesh=mesh,
        in_specs=(P("seq", "tp"), P("seq", "tp"), P("seq", "tp"), P(), P("tp", None)),
        out_specs=P("seq", "tp"),
        check_vma=False,
    )
```
